128 devices in a mesh: row: 8 (over x, y_hi), col: 16 (over z, y_lo, core).
Axes of the slice: x: 4, y: 4 (y_hi: 2, y_lo: 2; y = y_hi * 2 + y_lo), z: 4, core: 2. Of those that a mesh axis runs over, the one named last changes fastest.
Arguments:
- activations: bfloat16 [512, 28672], P('col', 'row'), may hold values from -6 to 6
- act_basis: bfloat16 [28672, 28672], P('row', 'col'), may hold values from -0.03125 to 0.03125
- out_grads: bfloat16 [512, 8192], P('row', 'col'), may hold values from -0.75 to 0.75
- grad_basis: bfloat16 [8192, 8192], P('col', 'row'), may hold values from -0.0625 to 0.0625
- lengths: int32 [8], replicated, may hold values from 1 to 128, 512 in all
Outputs:
- eigenvalues: float32 [8192, 28672], P('row', 'col')
The draws below stay inside these ranges and needn't reach their ends.
Inputs may be any that keep to these rules, and one draw needn't show every extreme that they name: `lengths`: each example has at least one token, the counts sum to 512, and the longest example has exactly 128 tokens.
All inputs are finite; a program needn't handle non-finite values.
Results may differ from the reference program's by a relative error of at most 0.0032.
Values may be sent and summed in bfloat16 or wider, within the bound.
A program may use at most 192 MiB of HBM per device.

```python
import math
import jax
import jax.numpy as jnp
import numpy as np
from jax import lax

D_IN = 28672
D_OUT = 8192
TOKENS = 512
EXAMPLES = 8
LEN_MAX = 128


def block_scale(rng, extent, shards, low, largest):
    factor_of, own = 1.0, jax.random.fold_in(rng, 6)
    for dim, parts in shards:
        draws = jnp.exp(jax.random.uniform(jax.random.fold_in(own, dim), (parts,), jnp.float32, low / len(shards), largest / len(shards)))
        factor_of = factor_of * jnp.repeat(draws, extent[dim] // parts).reshape([-1 if axis == dim else 1 for axis in range(len(extent))])
    return factor_of


def split_up(count, total, bound, lean):
    portions = [(1 << 20) // math.isqrt(grade ** lean) + 1 for grade in range(2, count + 1)]
    spare, holding = total - bound - (count - 1), [1] * (count - 1)
    while spare > 0:
        candidates = [i for i in range(count - 1) if holding[i] < bound]
        pool, remaining = sum([portions[i] for i in candidates]), spare
        for i in candidates:
            addition = min(bound - holding[i], max(1, remaining * portions[i] // pool), spare)
            holding[i] = holding[i] + addition
            spare = spare - addition
    return np.array([bound] + holding)


def ragged(key, count, total, limit, skew):
    if count == 2:
        one = jax.random.randint(key, (), max(1, total - limit), min(limit, total - 1) + 1)
        return jnp.stack([one, total - one])
    sizes = jnp.asarray(split_up(count, total, limit, skew), jnp.int32)
    twos = (count - 1) // 2
    donor, taker = sizes[1:1 + 2 * twos:2], sizes[2:2 + 2 * twos:2]
    slack = jnp.minimum(donor - 1, limit - taker)
    shifted = jax.random.randint(jax.random.fold_in(key, 1), (twos,), 0, 1 << 20) % (slack + 1)
    sizes = sizes.at[1:1 + 2 * twos:2].set(donor - shifted).at[2:2 + 2 * twos:2].set(taker + shifted)
    return sizes[jax.random.permutation(jax.random.fold_in(key, 2), count)]


def normal_values(own_key, dims, scale, limit, pieces=(), held_as=jnp.bfloat16):
    result = jax.random.normal(own_key, dims, jnp.float32) * scale
    if len(pieces) > 0:
        result = block_scale(own_key, dims, pieces, -0.22, 0.18) * result
    return jnp.clip(result, min=-limit, max=limit).astype(held_as)


def setup_inputs(seed: int = 0) -> dict:
    arg_keys = jax.random.split(jax.random.key(seed), 6)
    activations = normal_values(arg_keys[0], (TOKENS, D_IN), 1.0, 6.0, ((0, 16), (1, 8)))
    act_basis = normal_values(arg_keys[1], (D_IN, D_IN), D_IN ** -0.5, 0.03125, ((0, 8), (1, 16)))
    out_grads = normal_values(arg_keys[2], (TOKENS, D_OUT), 0.125, 0.75, ((0, 8), (1, 16)))
    grad_basis = normal_values(arg_keys[3], (D_OUT, D_OUT), D_OUT ** -0.5, 0.0625, ((0, 16), (1, 8)))
    lengths = ragged(arg_keys[4], EXAMPLES, TOKENS, LEN_MAX, 2).astype(jnp.int32)
    return dict(activations=activations, act_basis=act_basis, out_grads=out_grads, grad_basis=grad_basis, lengths=lengths)


def reference(activations, act_basis, out_grads, grad_basis, lengths):
    rotated_in = jnp.dot(activations, act_basis, preferred_element_type=jnp.float32).astype(jnp.bfloat16)
    rotated_out = jnp.dot(out_grads, grad_basis, preferred_element_type=jnp.float32).astype(jnp.bfloat16)
    example_ends = jnp.cumsum(lengths).astype(jnp.int32)
    example_starts = (example_ends - lengths).astype(jnp.int32)
    offsets = jnp.arange(LEN_MAX, dtype=jnp.int32)

    def accumulate(example, running_sum):
        first_token = example_starts[example]
        last_token = example_ends[example]
        window_start = jnp.minimum(first_token, TOKENS - LEN_MAX).astype(jnp.int32)
        rows_in = lax.dynamic_slice_in_dim(rotated_in, window_start, LEN_MAX, 0)
        rows_out = lax.dynamic_slice_in_dim(rotated_out, window_start, LEN_MAX, 0)
        token_index = window_start + offsets
        inside = (token_index >= first_token) & (token_index < last_token)
        rows_out = jnp.where(inside[:, None], rows_out, jnp.zeros_like(rows_out))
        product = lax.dot_general(rows_out, rows_in, (((0,), (0,)), ((), ())), preferred_element_type=jnp.float32)
        return running_sum + product * product

    running_sum = lax.fori_loop(0, EXAMPLES, accumulate, jnp.zeros((D_OUT, D_IN), jnp.float32))
    return running_sum * (1.0 / EXAMPLES)
```

```python
import functools

import jax
import jax.numpy as jnp
from jax import lax
from jax.experimental import pallas as pl
from jax.experimental.pallas import tpu as pltpu
from jax.sharding import PartitionSpec as P

MESH = pl.DeviceIdType.MESH
F32 = jnp.float32
BF16 = jnp.bfloat16

EXAMPLES = 8
TOKENS = 512
TILE = 256
WINDOW = 256
RING = 4
COPIES = 96


def rotate(
    act, basis, og, gbasis, rin_out, rout_out,
    a_full, b_v, pf, pb, relay_r, relay_l, direct_r, direct_l, mid_r, mid_l, total_r, total_l, sums, sums_b, y_in, rin,
    g_full, g_v, of, core_in, core_sum, o_relay_r, o_relay_l, o_direct_r, o_direct_l, o_mid_r, o_mid_l,
    o_total_r, o_total_l, o_sum, oy_in, rout,
    send_sem, recv_sem, load_sem, b_sem, store_sem,
):
    r, c = lax.axis_index("row"), lax.axis_index("col")
    x, yh = r // 2, r % 2
    z, yl, k = c // 4, (c // 2) % 2, c % 2
    features, width = a_full.shape[1], pf.shape[1]
    tiles = width // TILE

    def device(x=x, yh=yh, z=z, yl=yl, k=k):
        return (x * 2 + yh, z * 4 + yl * 2 + k)

    xn, xp, x2 = (x + 1) % RING, (x + 3) % RING, (x + 2) % RING
    zn, zp, z2 = (z + 1) % RING, (z + 3) % RING, (z + 2) % RING
    sib = device(k=1 - k)
    ylo = device(yl=1 - yl)
    yhi = device(yh=1 - yh)
    x_right, x_left = device(x=xn), device(x=xp)
    z_right, z_left = device(z=zn), device(z=zp)
    partners = (sib, ylo, yhi, x_right, x_left, z_right, z_left)

    copies = []

    def send(src, dst, to):
        i = len(copies)
        copy = pltpu.make_async_remote_copy(
            src_ref=src, dst_ref=dst, send_sem=send_sem.at[i], recv_sem=recv_sem.at[i], device_id=to, device_id_type=MESH
        )
        copy.start()
        copies.append(copy)
        return copy

    def rows(start, size):
        return pl.ds(pl.multiple_of(start, 16), size)

    own_rows = rows(c * 32, 32)
    loads = [
        pltpu.make_async_copy(act, a_full.at[own_rows], load_sem.at[0]),
        pltpu.make_async_copy(og, g_full.at[rows(r * 64, 64)], load_sem.at[1]),
        pltpu.make_async_copy(gbasis, g_v, load_sem.at[2]),
    ]
    for copy in loads[:2]:
        copy.start()

    def b_load(j):
        cols = pl.ds(pl.multiple_of(j * TILE, TILE), TILE)
        return pltpu.make_async_copy(basis.at[:, cols], b_v.at[:, cols], b_sem.at[j])

    for j in range(tiles):
        b_load(j).start()
    loads[2].start()

    barrier = pltpu.get_barrier_semaphore()
    for partner in partners:
        pl.semaphore_signal(barrier, inc=1, device_id=partner, device_id_type=MESH)
    pl.semaphore_wait(barrier, len(partners))

    def a_rows(z_, yl_, k_=k):
        return rows(z_ * 128 + yl_ * 64 + k_ * 32, 32)

    fhalf = features // 2

    def a_send(z_, yl_, to, half=None):
        where = (a_rows(z_, yl_),) if half is None else (a_rows(z_, yl_), pl.ds(half * fhalf, fhalf))
        return send(a_full.at[where], a_full.at[where], to)

    ghalf = og.shape[1] // 2

    def g_send(x_, yh_, to, half=None):
        where = (rows(x_ * 128 + yh_ * 64, 64),) if half is None else (rows(x_ * 128 + yh_ * 64, 64), pl.ds(half * ghalf, ghalf))
        return send(g_full.at[where], g_full.at[where], to)

    loads[0].wait()
    a_yl = a_send(z, yl, ylo)
    a_zr = a_send(z, yl, z_right)
    a_zl = a_send(z, yl, z_left)
    a_sib = [a_send(z, yl, sib)]
    loads[1].wait()
    g_y = g_send(x, yh, yhi)
    g_xr = g_send(x, yh, x_right)
    g_xl = g_send(x, yh, x_left)

    g_y.wait_recv()
    g2_xr = g_send(x, 1 - yh, x_right)
    g2_xl = g_send(x, 1 - yh, x_left)

    chunks = (
        (0, 64, z * 128 + yl * 64),
        (64, 64, z * 128 + (1 - yl) * 64),
        (128, 128, zp * 128),
        (256, 128, zn * 128),
        (384, 128, z2 * 128),
    )
    h0, h1 = pl.ds(0, width // 2), pl.ds(width // 2, width // 2)

    def multiply(n):
        first, size, token = chunks[n]

        def step(j, carry):
            if n == 0:
                b_load(j).wait()
            cols = pl.ds(pl.multiple_of(j * TILE, TILE), TILE)
            part = jnp.dot(a_full[rows(token, size), :], b_v[:, cols], preferred_element_type=F32)
            pf[first : first + size, cols] = part
            pb[first : first + size, cols] = part.astype(BF16)
            return carry

        lax.fori_loop(0, tiles, step, 0)

    state = [dict() for _ in chunks]

    def block(n, owner):
        first, size, _ = chunks[n]
        return rows(first + owner * (size // 4), size // 4)

    def land(n):
        first, size, _ = chunks[n]
        return pl.ds(first // 4, size // 4)

    def reduce_start(n):
        s, at = state[n], land(n)
        s["relay_r"] = send(pb.at[block(n, x2), h0], relay_r.at[at], x_right)
        s["relay_l"] = send(pb.at[block(n, x2), h1], relay_l.at[at], x_left)
        s["direct_r"] = send(pb.at[block(n, xn), h1], direct_r.at[at], x_right)
        s["direct_l"] = send(pb.at[block(n, xp), h0], direct_l.at[at], x_left)

    def reduce_mid(n):
        s, at = state[n], land(n)
        s["relay_r"].wait_recv()
        mid_r[at, :] = (pf[block(n, xn), h0] + relay_r[at, :].astype(F32)).astype(BF16)
        s["total_r"] = send(mid_r.at[at], total_r.at[at], x_right)
        s["relay_l"].wait_recv()
        mid_l[at, :] = (pf[block(n, xp), h1] + relay_l[at, :].astype(F32)).astype(BF16)
        s["total_l"] = send(mid_l.at[at], total_l.at[at], x_left)

    def reduce_end(n):
        s, at = state[n], land(n)
        s["direct_r"].wait_recv()
        s["direct_l"].wait_recv()
        s["total_r"].wait_recv()
        s["total_l"].wait_recv()
        sum0 = pf[block(n, x), h0] + direct_l[at, :].astype(F32) + total_r[at, :].astype(F32)
        sum1 = pf[block(n, x), h1] + direct_r[at, :].astype(F32) + total_l[at, :].astype(F32)
        sums[at, h0] = sum0
        sums[at, h1] = sum1
        sums_b[at, h0] = sum0.astype(BF16)
        sums_b[at, h1] = sum1.astype(BF16)
        s["y"] = send(sums_b.at[at], y_in.at[at], yhi)

    def tokens_of(n, owner):
        _, size, token = chunks[n]
        return rows(token + owner * (size // 4), size // 4)

    def gather_start(n):
        s, at = state[n], land(n)
        s["y"].wait_recv()
        mine = tokens_of(n, x)
        rin[mine, :] = (sums[at, :] + y_in[at, :].astype(F32)).astype(BF16)
        s["own_r"] = send(rin.at[mine], rin.at[mine], x_right)
        s["own_l"] = send(rin.at[mine], rin.at[mine], x_left)

    def gather_mid(n):
        s = state[n]
        s["own_r"].wait_recv()
        at = tokens_of(n, xp)
        s["far_r"] = send(rin.at[at, h0], rin.at[at, h0], x_right)
        s["own_l"].wait_recv()
        at = tokens_of(n, xn)
        s["far_l"] = send(rin.at[at, h1], rin.at[at, h1], x_left)

    stores = []

    def gather_end(n):
        s = state[n]
        s["far_r"].wait_recv()
        s["far_l"].wait_recv()
        _, size, token = chunks[n]
        at = rows(token, size)
        copy = pltpu.make_async_copy(rin.at[at], rin_out.at[at], store_sem.at[n])
        copy.start()
        stores.append(copy)

    multiply_first = functools.partial(multiply, 0)

    ohalf = of.shape[1] // 2
    o0, o1 = pl.ds(0, ohalf), pl.ds(ohalf, ohalf)
    o = {}

    def o_block(owner):
        return rows(owner * 64, 64)

    def out_multiply():
        of[...] = jnp.dot(g_full[...], g_v[...], preferred_element_type=F32)
        o["core"] = send(of.at[rows((1 - k) * 256, 256)], core_in, sib)

    def out_start():
        o["core"].wait_recv()
        core_sum[...] = of[rows(k * 256, 256), :] + core_in[...]
        o["relay_r"] = send(core_sum.at[o_block(z2), o0], o_relay_r, z_right)
        o["relay_l"] = send(core_sum.at[o_block(z2), o1], o_relay_l, z_left)
        o["direct_r"] = send(core_sum.at[o_block(zn), o1], o_direct_r, z_right)
        o["direct_l"] = send(core_sum.at[o_block(zp), o0], o_direct_l, z_left)

    def out_mid():
        o["relay_r"].wait_recv()
        o_mid_r[...] = core_sum[o_block(zn), o0] + o_relay_r[...]
        o["total_r"] = send(o_mid_r, o_total_r, z_right)
        o["relay_l"].wait_recv()
        o_mid_l[...] = core_sum[o_block(zp), o1] + o_relay_l[...]
        o["total_l"] = send(o_mid_l, o_total_l, z_left)

    def out_end():
        for name in ("direct_r", "direct_l", "total_r", "total_l"):
            o[name].wait_recv()
        o_sum[:, o0] = core_sum[o_block(z), o0] + o_direct_l[...] + o_total_r[...]
        o_sum[:, o1] = core_sum[o_block(z), o1] + o_direct_r[...] + o_total_l[...]
        o["y"] = send(o_sum, oy_in, ylo)

    def o_tokens(owner):
        return rows(k * 256 + owner * 64, 64)

    def out_gather_start():
        o["y"].wait_recv()
        mine = o_tokens(z)
        rout[mine, :] = (o_sum[...] + oy_in[...]).astype(BF16)
        o["own_r"] = send(rout.at[mine], rout.at[mine], z_right)
        o["own_l"] = send(rout.at[mine], rout.at[mine], z_left)

    def out_gather_mid():
        o["own_r"].wait_recv()
        at = o_tokens(zp)
        o["far_r"] = send(rout.at[at, o0], rout.at[at, o0], z_right)
        o["own_l"].wait_recv()
        at = o_tokens(zn)
        o["far_l"] = send(rout.at[at, o1], rout.at[at, o1], z_left)

    def out_gather_end():
        o["far_r"].wait_recv()
        o["far_l"].wait_recv()
        at = rows(k * 256, 256)
        o["sib"] = send(rout.at[at], rout.at[at], sib)

    def out_finish():
        o["sib"].wait_recv()
        copy = pltpu.make_async_copy(rout, rout_out, store_sem.at[len(chunks)])
        copy.start()
        stores.append(copy)

    a_sib[0].wait_recv()
    multiply_first()
    reduce_start(0)

    g_xr.wait_recv()
    g_far = [g_send(xp, yh, x_right, 0)]
    g_xl.wait_recv()
    g_far.append(g_send(xn, yh, x_left, 1))

    a_yl.wait_recv()
    a2_zr = a_send(z, 1 - yl, z_right)
    a2_zl = a_send(z, 1 - yl, z_left)
    a_sib_y = a_send(z, 1 - yl, sib)
    a_zr.wait_recv()
    a_far = [a_send(zp, yl, z_right, 0)]
    a_sib_l = [a_send(zp, yl, sib)]
    a_zl.wait_recv()
    a_far.append(a_send(zn, yl, z_left, 1))
    a_sib_r = [a_send(zn, yl, sib)]

    g2_xr.wait_recv()
    g_far.append(g_send(xp, 1 - yh, x_right, 0))
    g2_xl.wait_recv()
    g_far.append(g_send(xn, 1 - yh, x_left, 1))

    reduce_mid(0)
    a_sib_y.wait_recv()
    multiply(1)
    reduce_start(1)
    reduce_end(0)

    for copy in g_far:
        copy.wait_recv()
    loads[2].wait()
    out_multiply()

    a2_zr.wait_recv()
    a_far.append(a_send(zp, 1 - yl, z_right, 0))
    a_sib_l.append(a_send(zp, 1 - yl, sib))
    a2_zl.wait_recv()
    a_far.append(a_send(zn, 1 - yl, z_left, 1))
    a_sib_r.append(a_send(zn, 1 - yl, sib))

    reduce_mid(1)
    gather_start(0)
    out_start()
    for copy in a_sib_l:
        copy.wait_recv()
    multiply(2)
    reduce_start(2)
    reduce_end(1)
    gather_mid(0)
    for copy in a_sib_r:
        copy.wait_recv()
    multiply(3)
    reduce_start(3)
    a_sib_far = []
    for n, yl_ in enumerate((yl, 1 - yl)):
        for half in range(2):
            a_far[2 * n + half].wait_recv()
            a_sib_far.append(a_send(z2, yl_, sib, half))
    reduce_mid(2)
    gather_start(1)
    out_mid()
    for copy in a_sib_far:
        copy.wait_recv()
    multiply(4)
    reduce_start(4)
    reduce_mid(3)
    reduce_end(2)
    gather_mid(1)
    out_end()
    reduce_end(3)
    gather_start(2)
    reduce_mid(4)
    out_gather_start()
    gather_start(3)
    gather_mid(2)
    reduce_end(4)
    gather_mid(3)
    gather_start(4)
    out_gather_mid()
    gather_end(0)
    gather_end(1)
    out_gather_end()
    gather_end(2)
    gather_mid(4)
    gather_end(3)
    out_finish()
    gather_end(4)
    for copy in copies:
        copy.wait_send()
    for copy in stores:
        copy.wait()


def rotated(act, basis, og, gbasis):
    features, width = basis.shape
    o_features, o_width = gbasis.shape
    quarter = TOKENS // 4
    any_ = pl.BlockSpec(memory_space=pl.ANY)
    return pl.pallas_call(
        rotate,
        out_shape=(
            jax.ShapeDtypeStruct((TOKENS, width), BF16),
            jax.ShapeDtypeStruct((TOKENS, o_width), BF16),
        ),
        in_specs=[any_] * 4,
        out_specs=(any_, any_),
        scratch_shapes=[
            pltpu.VMEM((TOKENS, features), BF16),
            pltpu.VMEM((features, width), BF16),
            pltpu.VMEM((TOKENS, width), F32),
            pltpu.VMEM((TOKENS, width), BF16),
        ]
        + [pltpu.VMEM((quarter, width // 2), BF16)] * 8
        + [
            pltpu.VMEM((quarter, width), F32),
            pltpu.VMEM((quarter, width), BF16),
            pltpu.VMEM((quarter, width), BF16),
            pltpu.VMEM((TOKENS, width), BF16),
            pltpu.VMEM((TOKENS, o_features), BF16),
            pltpu.VMEM((o_features, o_width), BF16),
            pltpu.VMEM((TOKENS, o_width), F32),
            pltpu.VMEM((TOKENS // 2, o_width), F32),
            pltpu.VMEM((TOKENS // 2, o_width), F32),
        ]
        + [pltpu.VMEM((TOKENS // 8, o_width // 2), F32)] * 8
        + [
            pltpu.VMEM((TOKENS // 8, o_width), F32),
            pltpu.VMEM((TOKENS // 8, o_width), F32),
            pltpu.VMEM((TOKENS, o_width), BF16),
            pltpu.SemaphoreType.DMA((COPIES,)),
            pltpu.SemaphoreType.DMA((COPIES,)),
            pltpu.SemaphoreType.DMA((3,)),
            pltpu.SemaphoreType.DMA((width // TILE,)),
            pltpu.SemaphoreType.DMA((6,)),
        ],
        compiler_params=pltpu.CompilerParams(collective_id=0, has_side_effects=True, vmem_limit_bytes=56 << 20),
        name="rotate",
    )(act, basis, og, gbasis)


def square(lengths, rin, rout, out, acc, rout_t, out_sem):
    rout_t[...] = rout[...].T
    height, width = acc.shape
    firsts, lasts, starts = [], [], []
    end = jnp.int32(0)
    for e in range(EXAMPLES):
        firsts.append(end)
        starts.append(pl.multiple_of(jnp.minimum(end // 128 * 128, TOKENS - WINDOW), 128))
        end = end + lengths[e]
        lasts.append(end)
    token = lax.broadcasted_iota(jnp.int32, (WINDOW, TILE), 0)
    half = height // 2
    stores = []
    for j in range(width // TILE):
        cols = pl.ds(j * TILE, TILE)
        for m in range(2):
            at = pl.ds(m * half, half)
            total = jnp.zeros((half, TILE), F32)
            for e in range(EXAMPLES):
                inside = (token >= firsts[e] - starts[e]) & (token < lasts[e] - starts[e])
                window = rin[pl.ds(starts[e], WINDOW), cols]
                window = jnp.where(inside, window, jnp.zeros_like(window))
                product = jnp.dot(rout_t[at, pl.ds(starts[e], WINDOW)], window, preferred_element_type=F32)
                total = total + product * product
            acc[at, cols] = total * (1.0 / EXAMPLES)
        copy = pltpu.make_async_copy(acc.at[:, cols], out.at[:, cols], out_sem.at[j])
        copy.start()
        stores.append(copy)
    for copy in stores:
        copy.wait()


def squared(lengths, rin, rout):
    height, width = rout.shape[1], rin.shape[1]
    vmem = pl.BlockSpec(memory_space=pltpu.VMEM)
    return pl.pallas_call(
        square,
        out_shape=jax.ShapeDtypeStruct((height, width), F32),
        in_specs=[pl.BlockSpec(memory_space=pltpu.SMEM), vmem, vmem],
        out_specs=pl.BlockSpec(memory_space=pl.ANY),
        scratch_shapes=[
            pltpu.VMEM((height, width), F32),
            pltpu.VMEM((height, TOKENS), BF16),
            pltpu.SemaphoreType.DMA((width // TILE,)),
        ],
        compiler_params=pltpu.CompilerParams(vmem_limit_bytes=56 << 20),
        name="square",
    )(lengths, rin, rout)


def local(activations, act_basis, out_grads, grad_basis, lengths):
    rin, rout = rotated(activations, act_basis, out_grads, grad_basis)
    return squared(lengths, rin, rout)


def solution(mesh):
    return jax.shard_map(
        local,
        mesh=mesh,
        in_specs=(P("col", "row"), P("row", "col"), P("row", "col"), P("col", "row"), P()),
        out_specs=P("row", "col"),
        check_vma=False,
    )
```

```python
import functools

import jax
import jax.numpy as jnp
from jax import lax
from jax.experimental import pallas as pl
from jax.experimental.pallas import tpu as pltpu
from jax.sharding import PartitionSpec as P

MESH = pl.DeviceIdType.MESH
F32 = jnp.float32
BF16 = jnp.bfloat16

EXAMPLES = 8
TOKENS = 512
TILE = 256
WINDOW = 256
RING = 4
COPIES = 112


def rotate(
    act, basis, og, gbasis, rin_out, rout_out,
    a_full, b_v, pf, pb, relay_r, relay_l, direct_r, direct_l, mid_r, mid_l, total_r, total_l, sums, sums_b, y_in, rin,
    g_full, g_v, of, core_in, core_sum, o_relay_r, o_relay_l, o_direct_r, o_direct_l, o_mid_r, o_mid_l,
    o_total_r, o_total_l, o_sum, o_sum_b, oy_in, rout,
    send_sem, recv_sem, load_sem, b_sem, store_sem,
):
    r, c = lax.axis_index("row"), lax.axis_index("col")
    x, yh = r // 2, r % 2
    z, yl, k = c // 4, (c // 2) % 2, c % 2
    features, width = a_full.shape[1], pf.shape[1]
    tiles = width // TILE

    def device(x=x, yh=yh, z=z, yl=yl, k=k):
        return (x * 2 + yh, z * 4 + yl * 2 + k)

    xn, xp, x2 = (x + 1) % RING, (x + 3) % RING, (x + 2) % RING
    zn, zp, z2 = (z + 1) % RING, (z + 3) % RING, (z + 2) % RING
    sib = device(k=1 - k)
    ylo = device(yl=1 - yl)
    yhi = device(yh=1 - yh)
    x_right, x_left = device(x=xn), device(x=xp)
    z_right, z_left = device(z=zn), device(z=zp)
    partners = (sib, ylo, yhi, x_right, x_left, z_right, z_left)

    copies = []

    def send(src, dst, to):
        i = len(copies)
        copy = pltpu.make_async_remote_copy(
            src_ref=src, dst_ref=dst, send_sem=send_sem.at[i], recv_sem=recv_sem.at[i], device_id=to, device_id_type=MESH
        )
        copy.start()
        copies.append(copy)
        return copy

    def rows(start, size):
        return pl.ds(pl.multiple_of(start, 16), size)

    own_rows = rows(k * 32, 32)
    loads = [
        pltpu.make_async_copy(act, a_full.at[own_rows], load_sem.at[0]),
        pltpu.make_async_copy(og, g_full.at[rows(r * 64, 64)], load_sem.at[1]),
        pltpu.make_async_copy(gbasis, g_v, load_sem.at[2]),
    ]
    for copy in loads[:2]:
        copy.start()

    def b_load(j):
        cols = pl.ds(pl.multiple_of(j * TILE, TILE), TILE)
        return pltpu.make_async_copy(basis.at[:, cols], b_v.at[:, cols], b_sem.at[j])

    barrier = pltpu.get_barrier_semaphore()
    for partner in partners:
        pl.semaphore_signal(barrier, inc=1, device_id=partner, device_id_type=MESH)
    for copy in loads[:2]:
        copy.wait()
    for j in range(tiles):
        b_load(j).start()
    loads[2].start()
    pl.semaphore_wait(barrier, len(partners))

    OWN, PAIR, LOW, HIGH, LOW_PAIR, HIGH_PAIR, FAR, FAR_PAIR = range(8)
    fhalf = features // 2

    def a_send(source, target, to, half=None):
        cols = pl.ds(0, features) if half is None else pl.ds(half * fhalf, fhalf)
        return send(
            a_full.at[rows(source * 64 + k * 32, 32), cols], a_full.at[rows(target * 64 + k * 32, 32), cols], to
        )

    ghalf = og.shape[1] // 2

    def g_send(x_, yh_, to, half=None):
        where = (rows(x_ * 128 + yh_ * 64, 64),) if half is None else (rows(x_ * 128 + yh_ * 64, 64), pl.ds(half * ghalf, ghalf))
        return send(g_full.at[where], g_full.at[where], to)

    a_sib = a_send(OWN, OWN, sib)
    a_yl = a_send(OWN, PAIR, ylo)
    a_zr = a_send(OWN, LOW, z_right)
    a_zl = a_send(OWN, HIGH, z_left)
    g_y = g_send(x, yh, yhi)
    g_xr = g_send(x, yh, x_right)
    g_xl = g_send(x, yh, x_left)

    chunks = ((0, 64), (64, 64), (128, 128), (256, 128), (384, 64), (448, 64))
    h0, h1 = pl.ds(0, width // 2), pl.ds(width // 2, width // 2)

    def tokens_of(n, owner):
        if n in (0, 1):
            return rows(z * 128 + (yl + n) % 2 * 64 + owner * 16, 16)
        if n in (4, 5):
            return rows(z2 * 128 + (yl + n) % 2 * 64 + owner * 16, 16)
        return rows((z + 3 + owner // 2 * 2) % RING * 128 + (yl + n) % 2 * 64 + owner % 2 * 32, 32)

    def multiply(n, m=None):
        first = chunks[n][0]
        last = sum(chunks[n if m is None else m])

        def step(j, carry):
            if n == 0:
                b_load(j).wait()
            cols = pl.ds(pl.multiple_of(j * TILE, TILE), TILE)
            part = jnp.dot(a_full[first:last, :], b_v[:, cols], preferred_element_type=F32)
            pf[first:last, cols] = part
            pb[first:last, cols] = part.astype(BF16)
            return carry

        lax.fori_loop(0, tiles, step, 0)

    state = [dict() for _ in chunks]

    def block(n, owner):
        first, size = chunks[n]
        return rows(first + owner * (size // 4), size // 4)

    def land(n):
        first, size = chunks[n]
        return pl.ds(first // 4, size // 4)

    def reduce_start(n):
        s, at = state[n], land(n)
        s["relay_r"] = send(pb.at[block(n, x2), h0], relay_r.at[at], x_right)
        s["relay_l"] = send(pb.at[block(n, x2), h1], relay_l.at[at], x_left)
        s["direct_r"] = send(pb.at[block(n, xn), h1], direct_r.at[at], x_right)
        s["direct_l"] = send(pb.at[block(n, xp), h0], direct_l.at[at], x_left)

    def reduce_mid(n):
        s, at = state[n], land(n)
        s["relay_r"].wait_recv()
        mid_r[at, :] = (pf[block(n, xn), h0] + relay_r[at, :].astype(F32)).astype(BF16)
        s["total_r"] = send(mid_r.at[at], total_r.at[at], x_right)
        s["relay_l"].wait_recv()
        mid_l[at, :] = (pf[block(n, xp), h1] + relay_l[at, :].astype(F32)).astype(BF16)
        s["total_l"] = send(mid_l.at[at], total_l.at[at], x_left)

    def reduce_end(n):
        s, at = state[n], land(n)
        s["direct_r"].wait_recv()
        s["direct_l"].wait_recv()
        s["total_r"].wait_recv()
        s["total_l"].wait_recv()
        sum0 = pf[block(n, x), h0] + direct_l[at, :].astype(F32) + total_r[at, :].astype(F32)
        sum1 = pf[block(n, x), h1] + direct_r[at, :].astype(F32) + total_l[at, :].astype(F32)
        sums[at, h0] = sum0
        sums[at, h1] = sum1
        sums_b[at, h0] = sum0.astype(BF16)
        sums_b[at, h1] = sum1.astype(BF16)
        s["y"] = send(sums_b.at[at], y_in.at[at], yhi)

    def gather_start(n):
        s, at = state[n], land(n)
        s["y"].wait_recv()
        mine = tokens_of(n, x)
        rin[mine, :] = (sums[at, :] + y_in[at, :].astype(F32)).astype(BF16)
        s["own_r"] = send(rin.at[mine], rin.at[mine], x_right)
        s["own_l"] = send(rin.at[mine], rin.at[mine], x_left)

    def gather_mid(n):
        s = state[n]
        s["own_r"].wait_recv()
        at = tokens_of(n, xp)
        s["far_r"] = send(rin.at[at, h0], rin.at[at, h0], x_right)
        s["own_l"].wait_recv()
        at = tokens_of(n, xn)
        s["far_l"] = send(rin.at[at, h1], rin.at[at, h1], x_left)

    stores = []

    def gather_end(n):
        s = state[n]
        s["far_r"].wait_recv()
        s["far_l"].wait_recv()

    def store_rin():
        copy = pltpu.make_async_copy(rin, rin_out, store_sem.at[0])
        copy.start()
        stores.append(copy)

    ohalf = of.shape[1] // 2
    o0, o1 = pl.ds(0, ohalf), pl.ds(ohalf, ohalf)
    o = {}

    def o_block(owner):
        return rows(owner * 64, 64)

    def out_multiply():
        of[...] = jnp.dot(g_full[...], g_v[...], preferred_element_type=F32)
        o["core"] = send(of.at[rows((1 - k) * 256, 256)], core_in, sib)

    def out_start():
        o["core"].wait_recv()
        core_sum[...] = of[rows(k * 256, 256), :] + core_in[...]
        o["relay_r"] = send(core_sum.at[o_block(z2), o0], o_relay_r, z_right)
        o["relay_l"] = send(core_sum.at[o_block(z2), o1], o_relay_l, z_left)
        o["direct_r"] = send(core_sum.at[o_block(zn), o1], o_direct_r, z_right)
        o["direct_l"] = send(core_sum.at[o_block(zp), o0], o_direct_l, z_left)

    def out_mid():
        o["relay_r"].wait_recv()
        o_mid_r[...] = core_sum[o_block(zn), o0] + o_relay_r[...]
        o["total_r"] = send(o_mid_r, o_total_r, z_right)
        o["relay_l"].wait_recv()
        o_mid_l[...] = core_sum[o_block(zp), o1] + o_relay_l[...]
        o["total_l"] = send(o_mid_l, o_total_l, z_left)

    def out_end():
        for name in ("direct_r", "direct_l", "total_r", "total_l"):
            o[name].wait_recv()
        o_sum[:, o0] = core_sum[o_block(z), o0] + o_direct_l[...] + o_total_r[...]
        o_sum[:, o1] = core_sum[o_block(z), o1] + o_direct_r[...] + o_total_l[...]
        o_sum_b[...] = o_sum[...].astype(BF16)
        o["y"] = send(o_sum_b, oy_in, ylo)

    def o_tokens(owner):
        return rows(k * 256 + owner * 64, 64)

    def out_gather_start():
        o["y"].wait_recv()
        mine = o_tokens(z)
        rout[mine, :] = (o_sum[...] + oy_in[...].astype(F32)).astype(BF16)
        o["own_r"] = send(rout.at[mine], rout.at[mine], z_right)
        o["own_l"] = send(rout.at[mine], rout.at[mine], z_left)
        o["sib"] = [send(rout.at[mine], rout.at[mine], sib)]

    def out_gather_mid():
        o["own_r"].wait_recv()
        at = o_tokens(zp)
        o["far_r"] = send(rout.at[at, o0], rout.at[at, o0], z_right)
        o["sib"].append(send(rout.at[at], rout.at[at], sib))
        o["own_l"].wait_recv()
        at = o_tokens(zn)
        o["far_l"] = send(rout.at[at, o1], rout.at[at, o1], z_left)
        o["sib"].append(send(rout.at[at], rout.at[at], sib))

    def out_gather_end():
        at = o_tokens(z2)
        o["far_r"].wait_recv()
        o["sib"].append(send(rout.at[at, o0], rout.at[at, o0], sib))
        o["far_l"].wait_recv()
        o["sib"].append(send(rout.at[at, o1], rout.at[at, o1], sib))

    def out_finish():
        for copy in o["sib"]:
            copy.wait_recv()
        copy = pltpu.make_async_copy(rout, rout_out, store_sem.at[1])
        copy.start()
        stores.append(copy)

    a_sib.wait_recv()
    multiply(0)
    reduce_start(0)
    a_sib = {}
    a_zr.wait_recv()
    a_sib[2] = [a_send(LOW, LOW, sib)]
    a_far = [a_send(LOW, FAR, z_right, 0)]
    a_zl.wait_recv()
    a_sib[2].append(a_send(HIGH, HIGH, sib))
    a_far.append(a_send(HIGH, FAR, z_left, 1))
    g_xr.wait_recv()
    g_far = [g_send(xp, yh, x_right, 0)]
    g_xl.wait_recv()
    g_far.append(g_send(xn, yh, x_left, 1))
    a_yl.wait_recv()
    a_sib[1] = [a_send(PAIR, PAIR, sib)]
    a2_zr = a_send(PAIR, LOW_PAIR, z_right)
    a2_zl = a_send(PAIR, HIGH_PAIR, z_left)
    reduce_mid(0)
    g_y.wait_recv()
    g2_xr = g_send(x, 1 - yh, x_right)
    g2_xl = g_send(x, 1 - yh, x_left)
    for copy in a_sib[2]:
        copy.wait_recv()
    multiply(2)
    reduce_start(2)
    a_far[0].wait_recv()
    a_sib[4] = [a_send(FAR, FAR, sib, 0)]
    a_far[1].wait_recv()
    a_sib[4].append(a_send(FAR, FAR, sib, 1))
    g2_xr.wait_recv()
    g_far.append(g_send(xp, 1 - yh, x_right, 0))
    g2_xl.wait_recv()
    g_far.append(g_send(xn, 1 - yh, x_left, 1))
    for copy in a_sib[1]:
        copy.wait_recv()
    multiply(1)
    reduce_start(1)
    reduce_mid(2)
    a2_zr.wait_recv()
    a_sib[3] = [a_send(LOW_PAIR, LOW_PAIR, sib)]
    a_far2 = [a_send(LOW_PAIR, FAR_PAIR, z_right, 0)]
    a2_zl.wait_recv()
    a_sib[3].append(a_send(HIGH_PAIR, HIGH_PAIR, sib))
    a_far2.append(a_send(HIGH_PAIR, FAR_PAIR, z_left, 1))
    for copy in g_far:
        copy.wait_recv()
    loads[2].wait()
    out_multiply()
    for copy in a_sib[3]:
        copy.wait_recv()
    multiply(3)
    reduce_start(3)
    out_start()
    a_far2[0].wait_recv()
    a_sib[5] = [a_send(FAR_PAIR, FAR_PAIR, sib, 0)]
    a_far2[1].wait_recv()
    a_sib[5].append(a_send(FAR_PAIR, FAR_PAIR, sib, 1))
    reduce_end(0)
    reduce_mid(1)
    reduce_end(2)
    reduce_mid(3)
    for copy in a_sib[4]:
        copy.wait_recv()
    for copy in a_sib[5]:
        copy.wait_recv()
    multiply(4, 5)
    reduce_start(4)
    reduce_start(5)
    out_mid()
    reduce_end(3)
    reduce_end(1)
    gather_start(2)
    reduce_mid(5)
    gather_start(0)
    reduce_mid(4)
    out_end()
    gather_start(3)
    reduce_end(5)
    gather_start(1)
    gather_mid(2)
    reduce_end(4)
    out_gather_start()
    gather_mid(0)
    gather_start(5)
    gather_start(4)
    gather_mid(3)
    gather_mid(1)
    out_gather_mid()
    gather_end(2)
    gather_mid(5)
    gather_end(0)
    gather_mid(4)
    out_gather_end()
    gather_end(5)
    gather_end(3)
    gather_end(4)
    gather_end(1)
    store_rin()
    out_finish()
    for copy in copies:
        copy.wait_send()
    for copy in stores:
        copy.wait()


def rotated(act, basis, og, gbasis):
    features, width = basis.shape
    o_features, o_width = gbasis.shape
    quarter = TOKENS // 4
    any_ = pl.BlockSpec(memory_space=pl.ANY)
    return pl.pallas_call(
        rotate,
        out_shape=(
            jax.ShapeDtypeStruct((TOKENS, width), BF16),
            jax.ShapeDtypeStruct((TOKENS, o_width), BF16),
        ),
        in_specs=[any_] * 4,
        out_specs=(any_, any_),
        scratch_shapes=[
            pltpu.VMEM((TOKENS, features), BF16),
            pltpu.VMEM((features, width), BF16),
            pltpu.VMEM((TOKENS, width), F32),
            pltpu.VMEM((TOKENS, width), BF16),
        ]
        + [pltpu.VMEM((quarter, width // 2), BF16)] * 8
        + [
            pltpu.VMEM((quarter, width), F32),
            pltpu.VMEM((quarter, width), BF16),
            pltpu.VMEM((quarter, width), BF16),
            pltpu.VMEM((TOKENS, width), BF16),
            pltpu.VMEM((TOKENS, o_features), BF16),
            pltpu.VMEM((o_features, o_width), BF16),
            pltpu.VMEM((TOKENS, o_width), F32),
            pltpu.VMEM((TOKENS // 2, o_width), F32),
            pltpu.VMEM((TOKENS // 2, o_width), F32),
        ]
        + [pltpu.VMEM((TOKENS // 8, o_width // 2), F32)] * 8
        + [
            pltpu.VMEM((TOKENS // 8, o_width), F32),
            pltpu.VMEM((TOKENS // 8, o_width), BF16),
            pltpu.VMEM((TOKENS // 8, o_width), BF16),
            pltpu.VMEM((TOKENS, o_width), BF16),
            pltpu.SemaphoreType.DMA((COPIES,)),
            pltpu.SemaphoreType.DMA((COPIES,)),
            pltpu.SemaphoreType.DMA((3,)),
            pltpu.SemaphoreType.DMA((width // TILE,)),
            pltpu.SemaphoreType.DMA((2,)),
        ],
        compiler_params=pltpu.CompilerParams(collective_id=0, has_side_effects=True, vmem_limit_bytes=56 << 20),
        name="rotate",
    )(act, basis, og, gbasis)


def square(lengths, rin, rout, out, acc, rout_t, out_sem):
    rout_t[...] = rout[...].T
    height, width = acc.shape
    firsts, lasts, starts = [], [], []
    end = jnp.int32(0)
    for e in range(EXAMPLES):
        firsts.append(end)
        starts.append(pl.multiple_of(jnp.minimum(end // 128 * 128, TOKENS - WINDOW), 128))
        end = end + lengths[e]
        lasts.append(end)
    token = lax.broadcasted_iota(jnp.int32, (WINDOW, TILE), 0)
    half = height // 2
    stores = []
    for j in range(width // TILE):
        cols = pl.ds(j * TILE, TILE)
        for m in range(2):
            at = pl.ds(m * half, half)
            total = jnp.zeros((half, TILE), F32)
            for e in range(EXAMPLES):
                inside = (token >= firsts[e] - starts[e]) & (token < lasts[e] - starts[e])
                window = rin[pl.ds(starts[e], WINDOW), cols]
                window = jnp.where(inside, window, jnp.zeros_like(window))
                product = jnp.dot(rout_t[at, pl.ds(starts[e], WINDOW)], window, preferred_element_type=F32)
                total = total + product * product
            acc[at, cols] = total * (1.0 / EXAMPLES)
        copy = pltpu.make_async_copy(acc.at[:, cols], out.at[:, cols], out_sem.at[j])
        copy.start()
        stores.append(copy)
    for copy in stores:
        copy.wait()


def squared(lengths, rin, rout):
    height, width = rout.shape[1], rin.shape[1]
    vmem = pl.BlockSpec(memory_space=pltpu.VMEM)
    return pl.pallas_call(
        square,
        out_shape=jax.ShapeDtypeStruct((height, width), F32),
        in_specs=[pl.BlockSpec(memory_space=pltpu.SMEM), vmem, vmem],
        out_specs=pl.BlockSpec(memory_space=pl.ANY),
        scratch_shapes=[
            pltpu.VMEM((height, width), F32),
            pltpu.VMEM((height, TOKENS), BF16),
            pltpu.SemaphoreType.DMA((width // TILE,)),
        ],
        compiler_params=pltpu.CompilerParams(vmem_limit_bytes=56 << 20),
        name="square",
    )(lengths, rin, rout)


def local(activations, act_basis, out_grads, grad_basis, lengths):
    rin, rout = rotated(activations, act_basis, out_grads, grad_basis)
    return squared(lengths, rin, rout)


def solution(mesh):
    return jax.shard_map(
        local,
        mesh=mesh,
        in_specs=(P("col", "row"), P("row", "col"), P("row", "col"), P("col", "row"), P()),
        out_specs=P("row", "col"),
        check_vma=False,
    )
```

```python
import functools

import jax
import jax.numpy as jnp
from jax import lax
from jax.experimental import pallas as pl
from jax.experimental.pallas import tpu as pltpu
from jax.sharding import PartitionSpec as P

MESH = pl.DeviceIdType.MESH
F32 = jnp.float32
BF16 = jnp.bfloat16

EXAMPLES = 8
TOKENS = 512
TILE = 256
WINDOW = 256
RING = 4
COPIES = 112


def rotate(
    act, basis, og, gbasis, rin_out, rout_out,
    a_full, b_v, pf, pb, relay_r, relay_l, direct_r, direct_l, mid_r, mid_l, total_r, total_l, sums, sums_b, y_in, rin,
    g_full, g_v, of, core_in, core_sum, o_relay_r, o_relay_l, o_direct_r, o_direct_l, o_mid_r, o_mid_l,
    o_total_r, o_total_l, o_sum, o_sum_b, oy_in, rout,
    send_sem, recv_sem, load_sem, b_sem, store_sem,
):
    r, c = lax.axis_index("row"), lax.axis_index("col")
    x, yh = r // 2, r % 2
    z, yl, k = c // 4, (c // 2) % 2, c % 2
    features, width = a_full.shape[1], pf.shape[1]
    tiles = width // TILE

    def device(x=x, yh=yh, z=z, yl=yl, k=k):
        return (x * 2 + yh, z * 4 + yl * 2 + k)

    xn, xp, x2 = (x + 1) % RING, (x + 3) % RING, (x + 2) % RING
    zn, zp, z2 = (z + 1) % RING, (z + 3) % RING, (z + 2) % RING
    sib = device(k=1 - k)
    ylo = device(yl=1 - yl)
    yhi = device(yh=1 - yh)
    x_right, x_left = device(x=xn), device(x=xp)
    z_right, z_left = device(z=zn), device(z=zp)
    partners = (sib, ylo, yhi, x_right, x_left, z_right, z_left)

    copies = []

    def send(src, dst, to):
        i = len(copies)
        copy = pltpu.make_async_remote_copy(
            src_ref=src, dst_ref=dst, send_sem=send_sem.at[i], recv_sem=recv_sem.at[i], device_id=to, device_id_type=MESH
        )
        copy.start()
        copies.append(copy)
        return copy

    def rows(start, size):
        return pl.ds(pl.multiple_of(start, 16), size)

    own_rows = rows(k * 32, 32)
    loads = [
        pltpu.make_async_copy(act, a_full.at[own_rows], load_sem.at[0]),
        pltpu.make_async_copy(og, g_full.at[rows(r * 64, 64)], load_sem.at[1]),
        pltpu.make_async_copy(gbasis, g_v, load_sem.at[2]),
    ]
    for copy in loads[:2]:
        copy.start()

    def b_load(j):
        cols = pl.ds(pl.multiple_of(j * TILE, TILE), TILE)
        return pltpu.make_async_copy(basis.at[:, cols], b_v.at[:, cols], b_sem.at[j])

    barrier = pltpu.get_barrier_semaphore()
    for partner in partners:
        pl.semaphore_signal(barrier, inc=1, device_id=partner, device_id_type=MESH)
    for copy in loads[:2]:
        copy.wait()
    for j in range(tiles):
        b_load(j).start()
    loads[2].start()
    pl.semaphore_wait(barrier, len(partners))

    OWN, PAIR, LOW, HIGH, LOW_PAIR, HIGH_PAIR, FAR, FAR_PAIR = range(8)
    fhalf = features // 2

    def a_send(source, target, to, half=None):
        cols = pl.ds(0, features) if half is None else pl.ds(half * fhalf, fhalf)
        return send(
            a_full.at[rows(source * 64 + k * 32, 32), cols], a_full.at[rows(target * 64 + k * 32, 32), cols], to
        )

    ghalf = og.shape[1] // 2

    def g_send(x_, yh_, to, half=None):
        where = (rows(x_ * 128 + yh_ * 64, 64),) if half is None else (rows(x_ * 128 + yh_ * 64, 64), pl.ds(half * ghalf, ghalf))
        return send(g_full.at[where], g_full.at[where], to)

    a_sib = a_send(OWN, OWN, sib)
    a_yl = a_send(OWN, PAIR, ylo)
    a_zr = a_send(OWN, LOW, z_right)
    a_zl = a_send(OWN, HIGH, z_left)
    g_y = g_send(x, yh, yhi)
    g_xr = g_send(x, yh, x_right)
    g_xl = g_send(x, yh, x_left)

    chunks = ((0, 64), (64, 64), (128, 128), (256, 128), (384, 64), (448, 64))
    h0, h1 = pl.ds(0, width // 2), pl.ds(width // 2, width // 2)

    def tokens_of(n, owner):
        if n in (0, 1):
            return rows(z * 128 + (yl + n) % 2 * 64 + owner * 16, 16)
        if n in (4, 5):
            return rows(z2 * 128 + (yl + n) % 2 * 64 + owner * 16, 16)
        return rows((z + 3 + owner // 2 * 2) % RING * 128 + (yl + n) % 2 * 64 + owner % 2 * 32, 32)

    def multiply(n, m=None):
        first = chunks[n][0]
        last = sum(chunks[n if m is None else m])

        def step(j, carry):
            if n == 0:
                b_load(j).wait()
            cols = pl.ds(pl.multiple_of(j * TILE, TILE), TILE)
            part = jnp.dot(a_full[first:last, :], b_v[:, cols], preferred_element_type=F32)
            pf[first:last, cols] = part
            pb[first:last, cols] = part.astype(BF16)
            return carry

        lax.fori_loop(0, tiles, step, 0)

    state = [dict() for _ in chunks]

    def block(n, owner):
        first, size = chunks[n]
        return rows(first + owner * (size // 4), size // 4)

    def land(n):
        first, size = chunks[n]
        return pl.ds(first // 4, size // 4)

    def reduce_start(n):
        s, at = state[n], land(n)
        s["relay_r"] = send(pb.at[block(n, x2), h0], relay_r.at[at], x_right)
        s["relay_l"] = send(pb.at[block(n, x2), h1], relay_l.at[at], x_left)
        s["direct_r"] = send(pb.at[block(n, xn), h1], direct_r.at[at], x_right)
        s["direct_l"] = send(pb.at[block(n, xp), h0], direct_l.at[at], x_left)

    def reduce_mid(n):
        s, at = state[n], land(n)
        s["relay_r"].wait_recv()
        mid_r[at, :] = (pf[block(n, xn), h0] + relay_r[at, :].astype(F32)).astype(BF16)
        s["total_r"] = send(mid_r.at[at], total_r.at[at], x_right)
        s["relay_l"].wait_recv()
        mid_l[at, :] = (pf[block(n, xp), h1] + relay_l[at, :].astype(F32)).astype(BF16)
        s["total_l"] = send(mid_l.at[at], total_l.at[at], x_left)

    def reduce_end(n):
        s, at = state[n], land(n)
        s["direct_r"].wait_recv()
        s["direct_l"].wait_recv()
        s["total_r"].wait_recv()
        s["total_l"].wait_recv()
        sum0 = pf[block(n, x), h0] + direct_l[at, :].astype(F32) + total_r[at, :].astype(F32)
        sum1 = pf[block(n, x), h1] + direct_r[at, :].astype(F32) + total_l[at, :].astype(F32)
        sums[at, h0] = sum0
        sums[at, h1] = sum1
        sums_b[at, h0] = sum0.astype(BF16)
        sums_b[at, h1] = sum1.astype(BF16)
        s["y"] = send(sums_b.at[at], y_in.at[at], yhi)

    def gather_start(n):
        s, at = state[n], land(n)
        s["y"].wait_recv()
        mine = tokens_of(n, x)
        rin[mine, :] = (sums[at, :] + y_in[at, :].astype(F32)).astype(BF16)
        s["own_r"] = send(rin.at[mine], rin.at[mine], x_right)
        s["own_l"] = send(rin.at[mine], rin.at[mine], x_left)

    def gather_mid(n):
        s = state[n]
        s["own_r"].wait_recv()
        at = tokens_of(n, xp)
        s["far_r"] = send(rin.at[at, h0], rin.at[at, h0], x_right)
        s["own_l"].wait_recv()
        at = tokens_of(n, xn)
        s["far_l"] = send(rin.at[at, h1], rin.at[at, h1], x_left)

    stores = []

    def gather_end(n):
        s = state[n]
        s["far_r"].wait_recv()
        s["far_l"].wait_recv()

    def store_rin():
        copy = pltpu.make_async_copy(rin, rin_out, store_sem.at[0])
        copy.start()
        stores.append(copy)

    ohalf = of.shape[1] // 2
    o0, o1 = pl.ds(0, ohalf), pl.ds(ohalf, ohalf)
    o = {}

    def o_block(owner):
        return rows(owner * 64, 64)

    def out_multiply():
        of[...] = jnp.dot(g_full[...], g_v[...], preferred_element_type=F32)
        o["core"] = send(of.at[rows((1 - k) * 256, 256)], core_in, sib)

    def out_start():
        o["core"].wait_recv()
        core_sum[...] = of[rows(k * 256, 256), :] + core_in[...]
        o["relay_r"] = send(core_sum.at[o_block(z2), o0], o_relay_r, z_right)
        o["relay_l"] = send(core_sum.at[o_block(z2), o1], o_relay_l, z_left)
        o["direct_r"] = send(core_sum.at[o_block(zn), o1], o_direct_r, z_right)
        o["direct_l"] = send(core_sum.at[o_block(zp), o0], o_direct_l, z_left)

    def out_mid():
        o["relay_r"].wait_recv()
        o_mid_r[...] = core_sum[o_block(zn), o0] + o_relay_r[...]
        o["total_r"] = send(o_mid_r, o_total_r, z_right)
        o["relay_l"].wait_recv()
        o_mid_l[...] = core_sum[o_block(zp), o1] + o_relay_l[...]
        o["total_l"] = send(o_mid_l, o_total_l, z_left)

    def out_end():
        for name in ("direct_r", "direct_l", "total_r", "total_l"):
            o[name].wait_recv()
        o_sum[:, o0] = core_sum[o_block(z), o0] + o_direct_l[...] + o_total_r[...]
        o_sum[:, o1] = core_sum[o_block(z), o1] + o_direct_r[...] + o_total_l[...]
        o_sum_b[...] = o_sum[...].astype(BF16)
        o["y"] = send(o_sum_b, oy_in, ylo)

    def o_tokens(owner):
        return rows(k * 256 + owner * 64, 64)

    def out_gather_start():
        o["y"].wait_recv()
        mine = o_tokens(z)
        rout[mine, :] = (o_sum[...] + oy_in[...].astype(F32)).astype(BF16)
        o["own_r"] = send(rout.at[mine], rout.at[mine], z_right)
        o["own_l"] = send(rout.at[mine], rout.at[mine], z_left)
        o["sib"] = [send(rout.at[mine], rout.at[mine], sib)]

    def out_gather_mid():
        o["own_r"].wait_recv()
        at = o_tokens(zp)
        o["far_r"] = send(rout.at[at, o0], rout.at[at, o0], z_right)
        o["sib"].append(send(rout.at[at], rout.at[at], sib))
        o["own_l"].wait_recv()
        at = o_tokens(zn)
        o["far_l"] = send(rout.at[at, o1], rout.at[at, o1], z_left)
        o["sib"].append(send(rout.at[at], rout.at[at], sib))

    def out_gather_end():
        at = o_tokens(z2)
        o["far_r"].wait_recv()
        o["sib"].append(send(rout.at[at, o0], rout.at[at, o0], sib))
        o["far_l"].wait_recv()
        o["sib"].append(send(rout.at[at, o1], rout.at[at, o1], sib))

    def out_finish():
        for copy in o["sib"]:
            copy.wait_recv()
        copy = pltpu.make_async_copy(rout, rout_out, store_sem.at[1])
        copy.start()
        stores.append(copy)

    a_sib.wait_recv()
    multiply(0)
    reduce_start(0)
    a_sib = {}
    a_zr.wait_recv()
    a_sib[2] = [a_send(LOW, LOW, sib)]
    a_far = [a_send(LOW, FAR, z_right, 0)]
    a_zl.wait_recv()
    a_sib[2].append(a_send(HIGH, HIGH, sib))
    a_far.append(a_send(HIGH, FAR, z_left, 1))
    g_xr.wait_recv()
    g_far = [g_send(xp, yh, x_right, 0)]
    g_xl.wait_recv()
    g_far.append(g_send(xn, yh, x_left, 1))
    a_yl.wait_recv()
    a_sib[1] = [a_send(PAIR, PAIR, sib)]
    a2_zr = a_send(PAIR, LOW_PAIR, z_right)
    a2_zl = a_send(PAIR, HIGH_PAIR, z_left)
    reduce_mid(0)
    g_y.wait_recv()
    g2_xr = g_send(x, 1 - yh, x_right)
    g2_xl = g_send(x, 1 - yh, x_left)
    for copy in a_sib[2]:
        copy.wait_recv()
    multiply(2)
    reduce_start(2)
    a_far[0].wait_recv()
    a_sib[4] = [a_send(FAR, FAR, sib, 0)]
    a_far[1].wait_recv()
    a_sib[4].append(a_send(FAR, FAR, sib, 1))
    g2_xr.wait_recv()
    g_far.append(g_send(xp, 1 - yh, x_right, 0))
    g2_xl.wait_recv()
    g_far.append(g_send(xn, 1 - yh, x_left, 1))
    for copy in a_sib[1]:
        copy.wait_recv()
    multiply(1)
    reduce_start(1)
    reduce_mid(2)
    a2_zr.wait_recv()
    a_sib[3] = [a_send(LOW_PAIR, LOW_PAIR, sib)]
    a_far2 = [a_send(LOW_PAIR, FAR_PAIR, z_right, 0)]
    a2_zl.wait_recv()
    a_sib[3].append(a_send(HIGH_PAIR, HIGH_PAIR, sib))
    a_far2.append(a_send(HIGH_PAIR, FAR_PAIR, z_left, 1))
    for copy in g_far:
        copy.wait_recv()
    loads[2].wait()
    out_multiply()
    for copy in a_sib[3]:
        copy.wait_recv()
    multiply(3)
    reduce_start(3)
    out_start()
    a_far2[0].wait_recv()
    a_sib[5] = [a_send(FAR_PAIR, FAR_PAIR, sib, 0)]
    a_far2[1].wait_recv()
    a_sib[5].append(a_send(FAR_PAIR, FAR_PAIR, sib, 1))
    reduce_end(0)
    reduce_mid(1)
    reduce_end(2)
    reduce_mid(3)
    for copy in a_sib[4]:
        copy.wait_recv()
    for copy in a_sib[5]:
        copy.wait_recv()
    multiply(4, 5)
    reduce_start(4)
    reduce_start(5)
    out_mid()
    reduce_end(3)
    reduce_end(1)
    gather_start(2)
    reduce_mid(5)
    gather_start(0)
    reduce_mid(4)
    out_end()
    gather_start(3)
    reduce_end(5)
    gather_start(1)
    gather_mid(2)
    reduce_end(4)
    out_gather_start()
    gather_mid(0)
    gather_start(5)
    gather_start(4)
    gather_mid(3)
    gather_mid(1)
    out_gather_mid()
    gather_end(2)
    gather_mid(5)
    gather_end(0)
    gather_mid(4)
    out_gather_end()
    gather_end(5)
    gather_end(3)
    gather_end(4)
    gather_end(1)
    store_rin()
    out_finish()
    for copy in copies:
        copy.wait_send()
    for copy in stores:
        copy.wait()


def rotated(act, basis, og, gbasis):
    features, width = basis.shape
    o_features, o_width = gbasis.shape
    quarter = TOKENS // 4
    any_ = pl.BlockSpec(memory_space=pl.ANY)
    return pl.pallas_call(
        rotate,
        out_shape=(
            jax.ShapeDtypeStruct((TOKENS, width), BF16),
            jax.ShapeDtypeStruct((TOKENS, o_width), BF16),
        ),
        in_specs=[any_] * 4,
        out_specs=(any_, any_),
        scratch_shapes=[
            pltpu.VMEM((TOKENS, features), BF16),
            pltpu.VMEM((features, width), BF16),
            pltpu.VMEM((TOKENS, width), F32),
            pltpu.VMEM((TOKENS, width), BF16),
        ]
        + [pltpu.VMEM((quarter, width // 2), BF16)] * 8
        + [
            pltpu.VMEM((quarter, width), F32),
            pltpu.VMEM((quarter, width), BF16),
            pltpu.VMEM((quarter, width), BF16),
            pltpu.VMEM((TOKENS, width), BF16),
            pltpu.VMEM((TOKENS, o_features), BF16),
            pltpu.VMEM((o_features, o_width), BF16),
            pltpu.VMEM((TOKENS, o_width), F32),
            pltpu.VMEM((TOKENS // 2, o_width), F32),
            pltpu.VMEM((TOKENS // 2, o_width), F32),
        ]
        + [pltpu.VMEM((TOKENS // 8, o_width // 2), F32)] * 8
        + [
            pltpu.VMEM((TOKENS // 8, o_width), F32),
            pltpu.VMEM((TOKENS // 8, o_width), BF16),
            pltpu.VMEM((TOKENS // 8, o_width), BF16),
            pltpu.VMEM((TOKENS, o_width), BF16),
            pltpu.SemaphoreType.DMA((COPIES,)),
            pltpu.SemaphoreType.DMA((COPIES,)),
            pltpu.SemaphoreType.DMA((3,)),
            pltpu.SemaphoreType.DMA((width // TILE,)),
            pltpu.SemaphoreType.DMA((2,)),
        ],
        compiler_params=pltpu.CompilerParams(collective_id=0, has_side_effects=True, vmem_limit_bytes=56 << 20),
        name="rotate",
    )(act, basis, og, gbasis)


def square(lengths, rin, rout, out, acc, rout_t, masked, out_sem):
    rout_t[...] = rout[...].T
    height, width = acc.shape
    token = lax.broadcasted_iota(jnp.int32, (height, WINDOW), 1)
    starts = []
    last = jnp.int32(0)
    for e in range(EXAMPLES):
        first = last
        last = first + lengths[e]
        start = pl.multiple_of(jnp.minimum(first // 128 * 128, TOKENS - WINDOW), 128)
        window = rout_t[:, pl.ds(start, WINDOW)]
        inside = (token >= first - start) & (token < last - start)
        masked[e] = jnp.where(inside, window, jnp.zeros_like(window))
        starts.append(start)
    stores = []
    for j in range(width // TILE):
        cols = pl.ds(j * TILE, TILE)
        total = None
        for e in range(EXAMPLES):
            product = jnp.dot(masked[e], rin[pl.ds(starts[e], WINDOW), cols], preferred_element_type=F32)
            total = product * product if total is None else total + product * product
        acc[:, cols] = total * (1.0 / EXAMPLES)
        copy = pltpu.make_async_copy(acc.at[:, cols], out.at[:, cols], out_sem.at[j])
        copy.start()
        stores.append(copy)
    for copy in stores:
        copy.wait()


def squared(lengths, rin, rout):
    height, width = rout.shape[1], rin.shape[1]
    vmem = pl.BlockSpec(memory_space=pltpu.VMEM)
    return pl.pallas_call(
        square,
        out_shape=jax.ShapeDtypeStruct((height, width), F32),
        in_specs=[pl.BlockSpec(memory_space=pltpu.SMEM), vmem, vmem],
        out_specs=pl.BlockSpec(memory_space=pl.ANY),
        scratch_shapes=[
            pltpu.VMEM((height, width), F32),
            pltpu.VMEM((height, TOKENS), BF16),
            pltpu.VMEM((EXAMPLES, height, WINDOW), BF16),
            pltpu.SemaphoreType.DMA((width // TILE,)),
        ],
        compiler_params=pltpu.CompilerParams(vmem_limit_bytes=56 << 20),
        name="square",
    )(lengths, rin, rout)


def local(activations, act_basis, out_grads, grad_basis, lengths):
    rin, rout = rotated(activations, act_basis, out_grads, grad_basis)
    return squared(lengths, rin, rout)


def solution(mesh):
    return jax.shard_map(
        local,
        mesh=mesh,
        in_specs=(P("col", "row"), P("row", "col"), P("row", "col"), P("col", "row"), P()),
        out_specs=P("row", "col"),
        check_vma=False,
    )
```

```python
import functools

import jax
import jax.numpy as jnp
from jax import lax
from jax.experimental import pallas as pl
from jax.experimental.pallas import tpu as pltpu
from jax.sharding import PartitionSpec as P

MESH = pl.DeviceIdType.MESH
F32 = jnp.float32
BF16 = jnp.bfloat16

EXAMPLES = 8
TOKENS = 512
TILE = 256
WINDOW = 256
RING = 4
COPIES = 112


def rotate(
    act, basis, og, gbasis, rin_out, rout_out,
    a_full, b_v, pf, pb, relay_r, relay_l, direct_r, direct_l, mid_r, mid_l, total_r, total_l, sums, sums_b, y_in, rin,
    g_full, g_v, of, core_in, core_sum, o_relay_r, o_relay_l, o_direct_r, o_direct_l, o_mid_r, o_mid_l,
    o_total_r, o_total_l, o_sum, o_sum_b, oy_in, rout,
    send_sem, recv_sem, load_sem, b_sem, store_sem,
):
    r, c = lax.axis_index("row"), lax.axis_index("col")
    x, yh = r // 2, r % 2
    z, yl, k = c // 4, (c // 2) % 2, c % 2
    features, width = a_full.shape[1], pf.shape[1]
    tiles = width // TILE

    def device(x=x, yh=yh, z=z, yl=yl, k=k):
        return (x * 2 + yh, z * 4 + yl * 2 + k)

    xn, xp, x2 = (x + 1) % RING, (x + 3) % RING, (x + 2) % RING
    zn, zp, z2 = (z + 1) % RING, (z + 3) % RING, (z + 2) % RING
    sib = device(k=1 - k)
    ylo = device(yl=1 - yl)
    yhi = device(yh=1 - yh)
    x_right, x_left = device(x=xn), device(x=xp)
    z_right, z_left = device(z=zn), device(z=zp)
    partners = (sib, ylo, yhi, x_right, x_left, z_right, z_left)

    copies = []

    def send(src, dst, to):
        i = len(copies)
        copy = pltpu.make_async_remote_copy(
            src_ref=src, dst_ref=dst, send_sem=send_sem.at[i], recv_sem=recv_sem.at[i], device_id=to, device_id_type=MESH
        )
        copy.start()
        copies.append(copy)
        return copy

    def rows(start, size):
        return pl.ds(pl.multiple_of(start, 16), size)

    own_rows = rows(k * 32, 32)
    loads = [
        pltpu.make_async_copy(act, a_full.at[own_rows], load_sem.at[0]),
        pltpu.make_async_copy(og, g_full.at[rows(r * 64, 64)], load_sem.at[1]),
        pltpu.make_async_copy(gbasis, g_v, load_sem.at[2]),
    ]
    for copy in loads[:2]:
        copy.start()

    def b_load(j):
        cols = pl.ds(pl.multiple_of(j * TILE, TILE), TILE)
        return pltpu.make_async_copy(basis.at[:, cols], b_v.at[:, cols], b_sem.at[j])

    barrier = pltpu.get_barrier_semaphore()
    for partner in partners:
        pl.semaphore_signal(barrier, inc=1, device_id=partner, device_id_type=MESH)
    for copy in loads[:2]:
        copy.wait()
    for j in range(tiles):
        b_load(j).start()
    loads[2].start()
    pl.semaphore_wait(barrier, len(partners))

    OWN, PAIR, LOW, HIGH, LOW_PAIR, HIGH_PAIR, FAR, FAR_PAIR = range(8)
    fhalf = features // 2

    def a_send(source, target, to, half=None):
        cols = pl.ds(0, features) if half is None else pl.ds(half * fhalf, fhalf)
        return send(
            a_full.at[rows(source * 64 + k * 32, 32), cols], a_full.at[rows(target * 64 + k * 32, 32), cols], to
        )

    ghalf = og.shape[1] // 2

    def g_send(x_, yh_, to, half=None):
        where = (rows(x_ * 128 + yh_ * 64, 64),) if half is None else (rows(x_ * 128 + yh_ * 64, 64), pl.ds(half * ghalf, ghalf))
        return send(g_full.at[where], g_full.at[where], to)

    a_sib = a_send(OWN, OWN, sib)
    a_yl = a_send(OWN, PAIR, ylo)
    a_zr = a_send(OWN, LOW, z_right)
    a_zl = a_send(OWN, HIGH, z_left)
    g_y = g_send(x, yh, yhi)
    g_xr = g_send(x, yh, x_right)
    g_xl = g_send(x, yh, x_left)

    chunks = ((0, 64), (64, 64), (128, 128), (256, 128), (384, 64), (448, 64))
    h0, h1 = pl.ds(0, width // 2), pl.ds(width // 2, width // 2)

    def tokens_of(n, owner):
        if n in (0, 1):
            return rows(z * 128 + (yl + n) % 2 * 64 + owner * 16, 16)
        if n in (4, 5):
            return rows(z2 * 128 + (yl + n) % 2 * 64 + owner * 16, 16)
        return rows((z + 3 + owner // 2 * 2) % RING * 128 + (yl + n) % 2 * 64 + owner % 2 * 32, 32)

    def multiply(n, m=None):
        first = chunks[n][0]
        last = sum(chunks[n if m is None else m])

        def step(j, carry):
            if n == 0:
                b_load(j).wait()
            cols = pl.ds(pl.multiple_of(j * TILE, TILE), TILE)
            part = jnp.dot(a_full[first:last, :], b_v[:, cols], preferred_element_type=F32)
            pf[first:last, cols] = part
            pb[first:last, cols] = part.astype(BF16)
            return carry

        lax.fori_loop(0, tiles, step, 0)

    state = [dict() for _ in chunks]

    def block(n, owner):
        first, size = chunks[n]
        return rows(first + owner * (size // 4), size // 4)

    def land(n):
        first, size = chunks[n]
        return pl.ds(first // 4, size // 4)

    def reduce_start(n):
        s, at = state[n], land(n)
        s["relay_r"] = send(pb.at[block(n, x2), h0], relay_r.at[at], x_right)
        s["relay_l"] = send(pb.at[block(n, x2), h1], relay_l.at[at], x_left)
        s["direct_r"] = send(pb.at[block(n, xn), h1], direct_r.at[at], x_right)
        s["direct_l"] = send(pb.at[block(n, xp), h0], direct_l.at[at], x_left)

    def reduce_mid(n):
        s, at = state[n], land(n)
        s["relay_r"].wait_recv()
        mid_r[at, :] = (pf[block(n, xn), h0] + relay_r[at, :].astype(F32)).astype(BF16)
        s["total_r"] = send(mid_r.at[at], total_r.at[at], x_right)
        s["relay_l"].wait_recv()
        mid_l[at, :] = (pf[block(n, xp), h1] + relay_l[at, :].astype(F32)).astype(BF16)
        s["total_l"] = send(mid_l.at[at], total_l.at[at], x_left)

    def reduce_end(n):
        s, at = state[n], land(n)
        s["direct_r"].wait_recv()
        s["direct_l"].wait_recv()
        s["total_r"].wait_recv()
        s["total_l"].wait_recv()
        sum0 = pf[block(n, x), h0] + direct_l[at, :].astype(F32) + total_r[at, :].astype(F32)
        sum1 = pf[block(n, x), h1] + direct_r[at, :].astype(F32) + total_l[at, :].astype(F32)
        sums[at, h0] = sum0
        sums[at, h1] = sum1
        sums_b[at, h0] = sum0.astype(BF16)
        sums_b[at, h1] = sum1.astype(BF16)
        s["y"] = send(sums_b.at[at], y_in.at[at], yhi)

    def gather_start(n):
        s, at = state[n], land(n)
        s["y"].wait_recv()
        mine = tokens_of(n, x)
        rin[mine, :] = (sums[at, :] + y_in[at, :].astype(F32)).astype(BF16)
        s["own_r"] = send(rin.at[mine], rin.at[mine], x_right)
        s["own_l"] = send(rin.at[mine], rin.at[mine], x_left)

    def gather_mid(n):
        s = state[n]
        s["own_r"].wait_recv()
        at = tokens_of(n, xp)
        s["far_r"] = send(rin.at[at, h0], rin.at[at, h0], x_right)
        s["own_l"].wait_recv()
        at = tokens_of(n, xn)
        s["far_l"] = send(rin.at[at, h1], rin.at[at, h1], x_left)

    stores = []

    def gather_end(n):
        s = state[n]
        s["far_r"].wait_recv()
        s["far_l"].wait_recv()
        for piece in range(chunks[n][1] // 64):
            at = rows(tokens_of(n, 2 * piece).start, 64)
            copy = pltpu.make_async_copy(rin.at[at], rin_out.at[at], store_sem.at[len(stores)])
            copy.start()
            stores.append(copy)

    ohalf = of.shape[1] // 2
    o0, o1 = pl.ds(0, ohalf), pl.ds(ohalf, ohalf)
    o = {}

    def o_block(owner):
        return rows(owner * 64, 64)

    def out_multiply():
        of[...] = jnp.dot(g_full[...], g_v[...], preferred_element_type=F32)
        o["core"] = send(of.at[rows((1 - k) * 256, 256)], core_in, sib)

    def out_start():
        o["core"].wait_recv()
        core_sum[...] = of[rows(k * 256, 256), :] + core_in[...]
        o["relay_r"] = send(core_sum.at[o_block(z2), o0], o_relay_r, z_right)
        o["relay_l"] = send(core_sum.at[o_block(z2), o1], o_relay_l, z_left)
        o["direct_r"] = send(core_sum.at[o_block(zn), o1], o_direct_r, z_right)
        o["direct_l"] = send(core_sum.at[o_block(zp), o0], o_direct_l, z_left)

    def out_mid():
        o["relay_r"].wait_recv()
        o_mid_r[...] = core_sum[o_block(zn), o0] + o_relay_r[...]
        o["total_r"] = send(o_mid_r, o_total_r, z_right)
        o["relay_l"].wait_recv()
        o_mid_l[...] = core_sum[o_block(zp), o1] + o_relay_l[...]
        o["total_l"] = send(o_mid_l, o_total_l, z_left)

    def out_end():
        for name in ("direct_r", "direct_l", "total_r", "total_l"):
            o[name].wait_recv()
        o_sum[:, o0] = core_sum[o_block(z), o0] + o_direct_l[...] + o_total_r[...]
        o_sum[:, o1] = core_sum[o_block(z), o1] + o_direct_r[...] + o_total_l[...]
        o_sum_b[...] = o_sum[...].astype(BF16)
        o["y"] = send(o_sum_b, oy_in, ylo)

    def o_tokens(owner):
        return rows(k * 256 + owner * 64, 64)

    def out_gather_start():
        o["y"].wait_recv()
        mine = o_tokens(z)
        rout[mine, :] = (o_sum[...] + oy_in[...].astype(F32)).astype(BF16)
        o["own_r"] = send(rout.at[mine], rout.at[mine], z_right)
        o["own_l"] = send(rout.at[mine], rout.at[mine], z_left)
        o["sib"] = [send(rout.at[mine], rout.at[mine], sib)]

    def out_gather_mid():
        o["own_r"].wait_recv()
        at = o_tokens(zp)
        o["far_r"] = send(rout.at[at, o0], rout.at[at, o0], z_right)
        o["sib"].append(send(rout.at[at], rout.at[at], sib))
        o["own_l"].wait_recv()
        at = o_tokens(zn)
        o["far_l"] = send(rout.at[at, o1], rout.at[at, o1], z_left)
        o["sib"].append(send(rout.at[at], rout.at[at], sib))

    def out_gather_end():
        at = o_tokens(z2)
        o["far_r"].wait_recv()
        o["sib"].append(send(rout.at[at, o0], rout.at[at, o0], sib))
        o["far_l"].wait_recv()
        o["sib"].append(send(rout.at[at, o1], rout.at[at, o1], sib))

    def out_finish():
        for copy in o["sib"]:
            copy.wait_recv()
        copy = pltpu.make_async_copy(rout, rout_out, store_sem.at[len(stores)])
        copy.start()
        stores.append(copy)

    a_sib.wait_recv()
    multiply(0)
    reduce_start(0)
    a_sib = {}
    a_zr.wait_recv()
    a_sib[2] = [a_send(LOW, LOW, sib)]
    a_far = [a_send(LOW, FAR, z_right, 0)]
    a_zl.wait_recv()
    a_sib[2].append(a_send(HIGH, HIGH, sib))
    a_far.append(a_send(HIGH, FAR, z_left, 1))
    g_xr.wait_recv()
    g_far = [g_send(xp, yh, x_right, 0)]
    g_xl.wait_recv()
    g_far.append(g_send(xn, yh, x_left, 1))
    a_yl.wait_recv()
    a_sib[1] = [a_send(PAIR, PAIR, sib)]
    a2_zr = a_send(PAIR, LOW_PAIR, z_right)
    a2_zl = a_send(PAIR, HIGH_PAIR, z_left)
    reduce_mid(0)
    g_y.wait_recv()
    g2_xr = g_send(x, 1 - yh, x_right)
    g2_xl = g_send(x, 1 - yh, x_left)
    for copy in a_sib[2]:
        copy.wait_recv()
    multiply(2)
    reduce_start(2)
    a_far[0].wait_recv()
    a_sib[4] = [a_send(FAR, FAR, sib, 0)]
    a_far[1].wait_recv()
    a_sib[4].append(a_send(FAR, FAR, sib, 1))
    g2_xr.wait_recv()
    g_far.append(g_send(xp, 1 - yh, x_right, 0))
    g2_xl.wait_recv()
    g_far.append(g_send(xn, 1 - yh, x_left, 1))
    for copy in a_sib[1]:
        copy.wait_recv()
    multiply(1)
    reduce_start(1)
    reduce_mid(2)
    a2_zr.wait_recv()
    a_sib[3] = [a_send(LOW_PAIR, LOW_PAIR, sib)]
    a_far2 = [a_send(LOW_PAIR, FAR_PAIR, z_right, 0)]
    a2_zl.wait_recv()
    a_sib[3].append(a_send(HIGH_PAIR, HIGH_PAIR, sib))
    a_far2.append(a_send(HIGH_PAIR, FAR_PAIR, z_left, 1))
    for copy in g_far:
        copy.wait_recv()
    loads[2].wait()
    out_multiply()
    for copy in a_sib[3]:
        copy.wait_recv()
    multiply(3)
    reduce_start(3)
    out_start()
    a_far2[0].wait_recv()
    a_sib[5] = [a_send(FAR_PAIR, FAR_PAIR, sib, 0)]
    a_far2[1].wait_recv()
    a_sib[5].append(a_send(FAR_PAIR, FAR_PAIR, sib, 1))
    reduce_end(0)
    reduce_mid(1)
    reduce_end(2)
    reduce_mid(3)
    for copy in a_sib[4]:
        copy.wait_recv()
    for copy in a_sib[5]:
        copy.wait_recv()
    multiply(4, 5)
    reduce_start(4)
    reduce_start(5)
    out_mid()
    reduce_end(3)
    reduce_end(1)
    gather_start(2)
    reduce_mid(5)
    gather_start(0)
    reduce_mid(4)
    out_end()
    gather_start(3)
    reduce_end(5)
    gather_start(1)
    gather_mid(2)
    reduce_end(4)
    out_gather_start()
    gather_mid(0)
    gather_start(5)
    gather_start(4)
    gather_mid(3)
    gather_mid(1)
    out_gather_mid()
    gather_end(2)
    gather_mid(5)
    gather_end(0)
    gather_mid(4)
    out_gather_end()
    gather_end(5)
    gather_end(3)
    gather_end(4)
    gather_end(1)
    out_finish()
    for copy in copies:
        copy.wait_send()
    for copy in stores:
        copy.wait()


def rotated(act, basis, og, gbasis):
    features, width = basis.shape
    o_features, o_width = gbasis.shape
    quarter = TOKENS // 4
    any_ = pl.BlockSpec(memory_space=pl.ANY)
    return pl.pallas_call(
        rotate,
        out_shape=(
            jax.ShapeDtypeStruct((TOKENS, width), BF16),
            jax.ShapeDtypeStruct((TOKENS, o_width), BF16),
        ),
        in_specs=[any_] * 4,
        out_specs=(any_, any_),
        scratch_shapes=[
            pltpu.VMEM((TOKENS, features), BF16),
            pltpu.VMEM((features, width), BF16),
            pltpu.VMEM((TOKENS, width), F32),
            pltpu.VMEM((TOKENS, width), BF16),
        ]
        + [pltpu.VMEM((quarter, width // 2), BF16)] * 8
        + [
            pltpu.VMEM((quarter, width), F32),
            pltpu.VMEM((quarter, width), BF16),
            pltpu.VMEM((quarter, width), BF16),
            pltpu.VMEM((TOKENS, width), BF16),
            pltpu.VMEM((TOKENS, o_features), BF16),
            pltpu.VMEM((o_features, o_width), BF16),
            pltpu.VMEM((TOKENS, o_width), F32),
            pltpu.VMEM((TOKENS // 2, o_width), F32),
            pltpu.VMEM((TOKENS // 2, o_width), F32),
        ]
        + [pltpu.VMEM((TOKENS // 8, o_width // 2), F32)] * 8
        + [
            pltpu.VMEM((TOKENS // 8, o_width), F32),
            pltpu.VMEM((TOKENS // 8, o_width), BF16),
            pltpu.VMEM((TOKENS // 8, o_width), BF16),
            pltpu.VMEM((TOKENS, o_width), BF16),
            pltpu.SemaphoreType.DMA((COPIES,)),
            pltpu.SemaphoreType.DMA((COPIES,)),
            pltpu.SemaphoreType.DMA((3,)),
            pltpu.SemaphoreType.DMA((width // TILE,)),
            pltpu.SemaphoreType.DMA((9,)),
        ],
        compiler_params=pltpu.CompilerParams(collective_id=0, has_side_effects=True, vmem_limit_bytes=56 << 20),
        name="rotate",
    )(act, basis, og, gbasis)


def square(lengths, rin, rout, out, acc, rout_t, masked, out_sem):
    rout_t[...] = rout[...].T
    height, width = acc.shape
    token = lax.broadcasted_iota(jnp.int32, (height, WINDOW), 1)
    starts = []
    last = jnp.int32(0)
    for e in range(EXAMPLES):
        first = last
        last = first + lengths[e]
        start = pl.multiple_of(jnp.minimum(first // 128 * 128, TOKENS - WINDOW), 128)
        window = rout_t[:, pl.ds(start, WINDOW)]
        inside = (token >= first - start) & (token < last - start)
        masked[e] = jnp.where(inside, window, jnp.zeros_like(window))
        starts.append(start)
    stores = []
    for j in range(width // TILE):
        cols = pl.ds(j * TILE, TILE)
        total = None
        for e in range(EXAMPLES):
            product = jnp.dot(masked[e], rin[pl.ds(starts[e], WINDOW), cols], preferred_element_type=F32)
            total = product * product if total is None else total + product * product
        acc[:, cols] = total * (1.0 / EXAMPLES)
        copy = pltpu.make_async_copy(acc.at[:, cols], out.at[:, cols], out_sem.at[j])
        copy.start()
        stores.append(copy)
    for copy in stores:
        copy.wait()


def squared(lengths, rin, rout):
    height, width = rout.shape[1], rin.shape[1]
    vmem = pl.BlockSpec(memory_space=pltpu.VMEM)
    return pl.pallas_call(
        square,
        out_shape=jax.ShapeDtypeStruct((height, width), F32),
        in_specs=[pl.BlockSpec(memory_space=pltpu.SMEM), vmem, vmem],
        out_specs=pl.BlockSpec(memory_space=pl.ANY),
        scratch_shapes=[
            pltpu.VMEM((height, width), F32),
            pltpu.VMEM((height, TOKENS), BF16),
            pltpu.VMEM((EXAMPLES, height, WINDOW), BF16),
            pltpu.SemaphoreType.DMA((width // TILE,)),
        ],
        compiler_params=pltpu.CompilerParams(vmem_limit_bytes=56 << 20),
        name="square",
    )(lengths, rin, rout)


def local(activations, act_basis, out_grads, grad_basis, lengths):
    rin, rout = rotated(activations, act_basis, out_grads, grad_basis)
    return squared(lengths, rin, rout)


def solution(mesh):
    return jax.shard_map(
        local,
        mesh=mesh,
        in_specs=(P("col", "row"), P("row", "col"), P("row", "col"), P("col", "row"), P()),
        out_specs=P("row", "col"),
        check_vma=False,
    )
```

```python
import functools

import jax
import jax.numpy as jnp
from jax import lax
from jax.experimental import pallas as pl
from jax.experimental.pallas import tpu as pltpu
from jax.sharding import PartitionSpec as P

MESH = pl.DeviceIdType.MESH
F32 = jnp.float32
BF16 = jnp.bfloat16

EXAMPLES = 8
TOKENS = 512
TILE = 256
WINDOW = 256
RING = 4
COPIES = 112


def rotate(
    act, basis, og, gbasis, rin_out, rout_out,
    a_full, b_v, pf, pb, relay_r, relay_l, direct_r, direct_l, mid_r, mid_l, total_r, total_l, sums, sums_b, y_in, rin,
    g_full, g_v, of, core_in, core_sum, o_relay_r, o_relay_l, o_direct_r, o_direct_l, o_mid_r, o_mid_l,
    o_total_r, o_total_l, o_sum, o_sum_b, oy_in, rout,
    send_sem, recv_sem, load_sem, b_sem, store_sem,
):
    r, c = lax.axis_index("row"), lax.axis_index("col")
    x, yh = r // 2, r % 2
    z, yl, k = c // 4, (c // 2) % 2, c % 2
    features, width = a_full.shape[1], pf.shape[1]
    tiles = width // TILE

    def device(x=x, yh=yh, z=z, yl=yl, k=k):
        return (x * 2 + yh, z * 4 + yl * 2 + k)

    xn, xp, x2 = (x + 1) % RING, (x + 3) % RING, (x + 2) % RING
    zn, zp, z2 = (z + 1) % RING, (z + 3) % RING, (z + 2) % RING
    sib = device(k=1 - k)
    ylo = device(yl=1 - yl)
    yhi = device(yh=1 - yh)
    x_right, x_left = device(x=xn), device(x=xp)
    z_right, z_left = device(z=zn), device(z=zp)
    partners = (sib, ylo, yhi, x_right, x_left, z_right, z_left)

    copies = []

    def send(src, dst, to):
        i = len(copies)
        copy = pltpu.make_async_remote_copy(
            src_ref=src, dst_ref=dst, send_sem=send_sem.at[i], recv_sem=recv_sem.at[i], device_id=to, device_id_type=MESH
        )
        copy.start()
        copies.append(copy)
        return copy

    def rows(start, size):
        return pl.ds(pl.multiple_of(start, 16), size)

    own_rows = rows(k * 32, 32)
    loads = [
        pltpu.make_async_copy(act, a_full.at[own_rows], load_sem.at[0]),
        pltpu.make_async_copy(og, g_full.at[rows(r * 64, 64)], load_sem.at[1]),
        pltpu.make_async_copy(gbasis, g_v, load_sem.at[2]),
    ]
    for copy in loads[:2]:
        copy.start()

    def b_load(j):
        cols = pl.ds(pl.multiple_of(j * TILE, TILE), TILE)
        return pltpu.make_async_copy(basis.at[:, cols], b_v.at[:, cols], b_sem.at[j])

    barrier = pltpu.get_barrier_semaphore()
    for partner in partners:
        pl.semaphore_signal(barrier, inc=1, device_id=partner, device_id_type=MESH)
    for copy in loads[:2]:
        copy.wait()
    for j in range(tiles):
        b_load(j).start()
    loads[2].start()
    pl.semaphore_wait(barrier, len(partners))

    OWN, PAIR, LOW, HIGH, LOW_PAIR, HIGH_PAIR, FAR, FAR_PAIR = range(8)
    fhalf = features // 2

    def a_send(source, target, to, half=None):
        cols = pl.ds(0, features) if half is None else pl.ds(half * fhalf, fhalf)
        return send(
            a_full.at[rows(source * 64 + k * 32, 32), cols], a_full.at[rows(target * 64 + k * 32, 32), cols], to
        )

    ghalf = og.shape[1] // 2

    def g_send(x_, yh_, to, half=None):
        where = (rows(x_ * 128 + yh_ * 64, 64),) if half is None else (rows(x_ * 128 + yh_ * 64, 64), pl.ds(half * ghalf, ghalf))
        return send(g_full.at[where], g_full.at[where], to)

    a_sib = a_send(OWN, OWN, sib)
    a_yl = a_send(OWN, PAIR, ylo)
    a_zr = a_send(OWN, LOW, z_right)
    a_zl = a_send(OWN, HIGH, z_left)
    g_y = g_send(x, yh, yhi)
    g_xr = g_send(x, yh, x_right)
    g_xl = g_send(x, yh, x_left)

    chunks = ((0, 64), (64, 64), (128, 128), (256, 128), (384, 64), (448, 64))
    h0, h1 = pl.ds(0, width // 2), pl.ds(width // 2, width // 2)

    def tokens_of(n, owner):
        if n in (0, 1):
            return rows(z * 128 + (yl + n) % 2 * 64 + owner * 16, 16)
        if n in (4, 5):
            return rows(z2 * 128 + (yl + n) % 2 * 64 + owner * 16, 16)
        return rows((z + 3 + owner // 2 * 2) % RING * 128 + (yl + n) % 2 * 64 + owner % 2 * 32, 32)

    def multiply(n, m=None):
        first = chunks[n][0]
        last = sum(chunks[n if m is None else m])

        def step(j, carry):
            if n == 0:
                b_load(j).wait()
            cols = pl.ds(pl.multiple_of(j * TILE, TILE), TILE)
            part = jnp.dot(a_full[first:last, :], b_v[:, cols], preferred_element_type=F32)
            pf[first:last, cols] = part
            pb[first:last, cols] = part.astype(BF16)
            return carry

        lax.fori_loop(0, tiles, step, 0)

    state = [dict() for _ in chunks]

    def block(n, owner):
        first, size = chunks[n]
        return rows(first + owner * (size // 4), size // 4)

    def land(n):
        first, size = chunks[n]
        return pl.ds(first // 4, size // 4)

    def reduce_start(n):
        s, at = state[n], land(n)
        s["relay_r"] = send(pb.at[block(n, x2), h0], relay_r.at[at], x_right)
        s["relay_l"] = send(pb.at[block(n, x2), h1], relay_l.at[at], x_left)
        s["direct_r"] = send(pb.at[block(n, xn), h1], direct_r.at[at], x_right)
        s["direct_l"] = send(pb.at[block(n, xp), h0], direct_l.at[at], x_left)

    def reduce_mid(n):
        s, at = state[n], land(n)
        s["relay_r"].wait_recv()
        mid_r[at, :] = (pf[block(n, xn), h0] + relay_r[at, :].astype(F32)).astype(BF16)
        s["total_r"] = send(mid_r.at[at], total_r.at[at], x_right)
        s["relay_l"].wait_recv()
        mid_l[at, :] = (pf[block(n, xp), h1] + relay_l[at, :].astype(F32)).astype(BF16)
        s["total_l"] = send(mid_l.at[at], total_l.at[at], x_left)

    def reduce_end(n):
        s, at = state[n], land(n)
        s["direct_r"].wait_recv()
        s["direct_l"].wait_recv()
        s["total_r"].wait_recv()
        s["total_l"].wait_recv()
        sum0 = pf[block(n, x), h0] + direct_l[at, :].astype(F32) + total_r[at, :].astype(F32)
        sum1 = pf[block(n, x), h1] + direct_r[at, :].astype(F32) + total_l[at, :].astype(F32)
        sums[at, h0] = sum0
        sums[at, h1] = sum1
        sums_b[at, h0] = sum0.astype(BF16)
        sums_b[at, h1] = sum1.astype(BF16)
        s["y"] = send(sums_b.at[at], y_in.at[at], yhi)

    def gather_start(n):
        s, at = state[n], land(n)
        s["y"].wait_recv()
        mine = tokens_of(n, x)
        rin[mine, :] = (sums[at, :] + y_in[at, :].astype(F32)).astype(BF16)
        s["own_r"] = send(rin.at[mine], rin.at[mine], x_right)
        s["own_l"] = send(rin.at[mine], rin.at[mine], x_left)

    def gather_mid(n):
        s = state[n]
        s["own_r"].wait_recv()
        at = tokens_of(n, xp)
        s["far_r"] = send(rin.at[at, h0], rin.at[at, h0], x_right)
        s["own_l"].wait_recv()
        at = tokens_of(n, xn)
        s["far_l"] = send(rin.at[at, h1], rin.at[at, h1], x_left)

    stores = []

    def gather_end(n):
        s = state[n]
        s["far_r"].wait_recv()
        s["far_l"].wait_recv()
        for piece in range(chunks[n][1] // 64):
            at = rows(tokens_of(n, 2 * piece).start, 64)
            copy = pltpu.make_async_copy(rin.at[at], rin_out.at[at], store_sem.at[len(stores)])
            copy.start()
            stores.append(copy)

    ohalf = of.shape[1] // 2
    o0, o1 = pl.ds(0, ohalf), pl.ds(ohalf, ohalf)
    o = {}

    def o_block(owner):
        return rows(owner * 64, 64)

    def out_multiply():
        of[...] = jnp.dot(g_full[...], g_v[...], preferred_element_type=F32)
        o["core"] = send(of.at[rows((1 - k) * 256, 256)], core_in, sib)

    def out_start():
        o["core"].wait_recv()
        core_sum[...] = of[rows(k * 256, 256), :] + core_in[...]
        o["relay_r"] = send(core_sum.at[o_block(z2), o0], o_relay_r, z_right)
        o["relay_l"] = send(core_sum.at[o_block(z2), o1], o_relay_l, z_left)
        o["direct_r"] = send(core_sum.at[o_block(zn), o1], o_direct_r, z_right)
        o["direct_l"] = send(core_sum.at[o_block(zp), o0], o_direct_l, z_left)

    def out_mid():
        o["relay_r"].wait_recv()
        o_mid_r[...] = core_sum[o_block(zn), o0] + o_relay_r[...]
        o["total_r"] = send(o_mid_r, o_total_r, z_right)
        o["relay_l"].wait_recv()
        o_mid_l[...] = core_sum[o_block(zp), o1] + o_relay_l[...]
        o["total_l"] = send(o_mid_l, o_total_l, z_left)

    def out_end():
        for name in ("direct_r", "direct_l", "total_r", "total_l"):
            o[name].wait_recv()
        o_sum[:, o0] = core_sum[o_block(z), o0] + o_direct_l[...] + o_total_r[...]
        o_sum[:, o1] = core_sum[o_block(z), o1] + o_direct_r[...] + o_total_l[...]
        o_sum_b[...] = o_sum[...].astype(BF16)
        o["y"] = send(o_sum_b, oy_in, ylo)

    def o_tokens(owner):
        return rows(k * 256 + owner * 64, 64)

    def out_gather_start():
        o["y"].wait_recv()
        mine = o_tokens(z)
        rout[mine, :] = (o_sum[...] + oy_in[...].astype(F32)).astype(BF16)
        o["own_r"] = send(rout.at[mine], rout.at[mine], z_right)
        o["own_l"] = send(rout.at[mine], rout.at[mine], z_left)
        o["sib"] = [send(rout.at[mine], rout.at[mine], sib)]

    def out_gather_mid():
        o["own_r"].wait_recv()
        at = o_tokens(zp)
        o["far_r"] = send(rout.at[at, o0], rout.at[at, o0], z_right)
        o["sib"].append(send(rout.at[at], rout.at[at], sib))
        o["own_l"].wait_recv()
        at = o_tokens(zn)
        o["far_l"] = send(rout.at[at, o1], rout.at[at, o1], z_left)
        o["sib"].append(send(rout.at[at], rout.at[at], sib))

    def out_gather_end():
        at = o_tokens(z2)
        o["far_r"].wait_recv()
        o["sib"].append(send(rout.at[at, o0], rout.at[at, o0], sib))
        o["far_l"].wait_recv()
        o["sib"].append(send(rout.at[at, o1], rout.at[at, o1], sib))

    def out_finish():
        for half in (k, 1 - k):
            if half is not k:
                for copy in o["sib"]:
                    copy.wait_recv()
            at = rows(half * 256, 256)
            copy = pltpu.make_async_copy(rout.at[at], rout_out.at[at], store_sem.at[len(stores)])
            copy.start()
            stores.append(copy)

    a_sib.wait_recv()
    multiply(0)
    reduce_start(0)
    a_sib = {}
    a_zr.wait_recv()
    a_sib[2] = [a_send(LOW, LOW, sib)]
    a_far = [a_send(LOW, FAR, z_right, 0)]
    a_zl.wait_recv()
    a_sib[2].append(a_send(HIGH, HIGH, sib))
    a_far.append(a_send(HIGH, FAR, z_left, 1))
    g_xr.wait_recv()
    g_far = [g_send(xp, yh, x_right, 0)]
    g_xl.wait_recv()
    g_far.append(g_send(xn, yh, x_left, 1))
    a_yl.wait_recv()
    a_sib[1] = [a_send(PAIR, PAIR, sib)]
    a2_zr = a_send(PAIR, LOW_PAIR, z_right)
    a2_zl = a_send(PAIR, HIGH_PAIR, z_left)
    reduce_mid(0)
    g_y.wait_recv()
    g2_xr = g_send(x, 1 - yh, x_right)
    g2_xl = g_send(x, 1 - yh, x_left)
    for copy in a_sib[2]:
        copy.wait_recv()
    multiply(2)
    reduce_start(2)
    a_far[0].wait_recv()
    a_sib[4] = [a_send(FAR, FAR, sib, 0)]
    a_far[1].wait_recv()
    a_sib[4].append(a_send(FAR, FAR, sib, 1))
    g2_xr.wait_recv()
    g_far.append(g_send(xp, 1 - yh, x_right, 0))
    g2_xl.wait_recv()
    g_far.append(g_send(xn, 1 - yh, x_left, 1))
    for copy in a_sib[1]:
        copy.wait_recv()
    multiply(1)
    reduce_start(1)
    reduce_mid(2)
    a2_zr.wait_recv()
    a_sib[3] = [a_send(LOW_PAIR, LOW_PAIR, sib)]
    a_far2 = [a_send(LOW_PAIR, FAR_PAIR, z_right, 0)]
    a2_zl.wait_recv()
    a_sib[3].append(a_send(HIGH_PAIR, HIGH_PAIR, sib))
    a_far2.append(a_send(HIGH_PAIR, FAR_PAIR, z_left, 1))
    for copy in g_far:
        copy.wait_recv()
    loads[2].wait()
    out_multiply()
    for copy in a_sib[3]:
        copy.wait_recv()
    multiply(3)
    reduce_start(3)
    out_start()
    a_far2[0].wait_recv()
    a_sib[5] = [a_send(FAR_PAIR, FAR_PAIR, sib, 0)]
    a_far2[1].wait_recv()
    a_sib[5].append(a_send(FAR_PAIR, FAR_PAIR, sib, 1))
    reduce_end(0)
    reduce_mid(1)
    reduce_end(2)
    reduce_mid(3)
    for copy in a_sib[4]:
        copy.wait_recv()
    for copy in a_sib[5]:
        copy.wait_recv()
    multiply(4, 5)
    reduce_start(4)
    reduce_start(5)
    out_mid()
    reduce_end(3)
    reduce_end(1)
    gather_start(2)
    reduce_mid(5)
    gather_start(0)
    reduce_mid(4)
    out_end()
    gather_start(3)
    reduce_end(5)
    gather_start(1)
    gather_mid(2)
    reduce_end(4)
    out_gather_start()
    gather_mid(0)
    gather_start(5)
    gather_start(4)
    gather_mid(3)
    gather_mid(1)
    out_gather_mid()
    gather_end(2)
    gather_mid(5)
    gather_end(0)
    gather_mid(4)
    out_gather_end()
    gather_end(5)
    gather_end(3)
    gather_end(4)
    gather_end(1)
    out_finish()
    for copy in copies:
        copy.wait_send()
    for copy in stores:
        copy.wait()


def rotated(act, basis, og, gbasis):
    features, width = basis.shape
    o_features, o_width = gbasis.shape
    quarter = TOKENS // 4
    any_ = pl.BlockSpec(memory_space=pl.ANY)
    return pl.pallas_call(
        rotate,
        out_shape=(
            jax.ShapeDtypeStruct((TOKENS, width), BF16),
            jax.ShapeDtypeStruct((TOKENS, o_width), BF16),
        ),
        in_specs=[any_] * 4,
        out_specs=(any_, any_),
        scratch_shapes=[
            pltpu.VMEM((TOKENS, features), BF16),
            pltpu.VMEM((features, width), BF16),
            pltpu.VMEM((TOKENS, width), F32),
            pltpu.VMEM((TOKENS, width), BF16),
        ]
        + [pltpu.VMEM((quarter, width // 2), BF16)] * 8
        + [
            pltpu.VMEM((quarter, width), F32),
            pltpu.VMEM((quarter, width), BF16),
            pltpu.VMEM((quarter, width), BF16),
            pltpu.VMEM((TOKENS, width), BF16),
            pltpu.VMEM((TOKENS, o_features), BF16),
            pltpu.VMEM((o_features, o_width), BF16),
            pltpu.VMEM((TOKENS, o_width), F32),
            pltpu.VMEM((TOKENS // 2, o_width), F32),
            pltpu.VMEM((TOKENS // 2, o_width), F32),
        ]
        + [pltpu.VMEM((TOKENS // 8, o_width // 2), F32)] * 8
        + [
            pltpu.VMEM((TOKENS // 8, o_width), F32),
            pltpu.VMEM((TOKENS // 8, o_width), BF16),
            pltpu.VMEM((TOKENS // 8, o_width), BF16),
            pltpu.VMEM((TOKENS, o_width), BF16),
            pltpu.SemaphoreType.DMA((COPIES,)),
            pltpu.SemaphoreType.DMA((COPIES,)),
            pltpu.SemaphoreType.DMA((3,)),
            pltpu.SemaphoreType.DMA((width // TILE,)),
            pltpu.SemaphoreType.DMA((10,)),
        ],
        compiler_params=pltpu.CompilerParams(collective_id=0, has_side_effects=True, vmem_limit_bytes=56 << 20),
        name="rotate",
    )(act, basis, og, gbasis)


def square(lengths, rin, rout, out, acc, rout_t, masked, out_sem):
    rout_t[...] = rout[...].T
    height, width = acc.shape
    token = lax.broadcasted_iota(jnp.int32, (height, WINDOW), 1)
    starts = []
    last = jnp.int32(0)
    for e in range(EXAMPLES):
        first = last
        last = first + lengths[e]
        start = pl.multiple_of(jnp.minimum(first // 128 * 128, TOKENS - WINDOW), 128)
        window = rout_t[:, pl.ds(start, WINDOW)]
        inside = (token >= first - start) & (token < last - start)
        masked[e] = jnp.where(inside, window, jnp.zeros_like(window))
        starts.append(start)
    stores = []
    for j in range(width // TILE):
        cols = pl.ds(j * TILE, TILE)
        total = None
        for e in range(EXAMPLES):
            product = jnp.dot(masked[e], rin[pl.ds(starts[e], WINDOW), cols], preferred_element_type=F32)
            total = product * product if total is None else total + product * product
        acc[:, cols] = total * (1.0 / EXAMPLES)
        copy = pltpu.make_async_copy(acc.at[:, cols], out.at[:, cols], out_sem.at[j])
        copy.start()
        stores.append(copy)
    for copy in stores:
        copy.wait()


def squared(lengths, rin, rout):
    height, width = rout.shape[1], rin.shape[1]
    vmem = pl.BlockSpec(memory_space=pltpu.VMEM)
    return pl.pallas_call(
        square,
        out_shape=jax.ShapeDtypeStruct((height, width), F32),
        in_specs=[pl.BlockSpec(memory_space=pltpu.SMEM), vmem, vmem],
        out_specs=pl.BlockSpec(memory_space=pl.ANY),
        scratch_shapes=[
            pltpu.VMEM((height, width), F32),
            pltpu.VMEM((height, TOKENS), BF16),
            pltpu.VMEM((EXAMPLES, height, WINDOW), BF16),
            pltpu.SemaphoreType.DMA((width // TILE,)),
        ],
        compiler_params=pltpu.CompilerParams(vmem_limit_bytes=56 << 20),
        name="square",
    )(lengths, rin, rout)


def local(activations, act_basis, out_grads, grad_basis, lengths):
    rin, rout = rotated(activations, act_basis, out_grads, grad_basis)
    return squared(lengths, rin, rout)


def solution(mesh):
    return jax.shard_map(
        local,
        mesh=mesh,
        in_specs=(P("col", "row"), P("row", "col"), P("row", "col"), P("col", "row"), P()),
        out_specs=P("row", "col"),
        check_vma=False,
    )
```
